32 devices in a mesh: rows: 4 (over z), cols: 8 (over y, x, core).
Axes of the slice: x: 2, y: 2, z: 4, core: 2. Of those that a mesh axis runs over, the one named last changes fastest.
Arguments:
- momentum_prev: float32 [8192, 8192], P('rows', 'cols'), may hold values from -170 to 170
- gradient: bfloat16 [8192, 8192], P('rows', 'cols'), may hold values from -6 to 6
- q_prev: float32 [8192, 512], P('cols'), may hold values from -0.0625 to 0.0625
Outputs:
- momentum_next: float32 [8192, 8192], P('rows', 'cols')
- q_next: float32 [8192, 512], P('cols')
- update: bfloat16 [8192, 8192], P('rows', 'cols')
The draws below stay inside these ranges and needn't reach their ends.
All inputs are finite; a program needn't handle non-finite values.
Results may differ from the reference program's by a relative error of at most 0.001.
Values sent between devices are 32-bit elements; how exact they have to be, the bound alone decides.
No kernel may reach another device: no remote copies, remote signals or barrier semaphores. Data moves between devices by JAX's collectives and lax.ppermute only.
A program may use at most 128 MiB of HBM per device.

```python
import math
import jax
import jax.numpy as jnp
from jax import lax

D = 8192
RANK = 512


def draw_momentum_prev(key, part):
    key_base = jax.random.fold_in(key, 11)
    key_rows = jax.random.fold_in(key, 12)
    key_cols = jax.random.fold_in(key, 13)
    row_scale = jnp.exp(jax.random.uniform(key_rows, (D, 1), jnp.float32, 0.0, math.log(3.0)))
    col_scale = jnp.exp(jax.random.uniform(key_cols, (1, D), jnp.float32, 0.0, math.log(3.0)))
    rising = jnp.power(3.0, jnp.arange(D, dtype=jnp.float32) / D)[None, :]
    base = jnp.clip(jax.random.normal(key_base, (D, D), jnp.float32), -6.0, 6.0)
    return base * row_scale * col_scale * rising


def shard_levels(own_key, dims, split, low, high):
    factor_of, own = 1.0, jax.random.fold_in(own_key, 6)
    for position, parts in split:
        draws = jnp.exp(jax.random.uniform(jax.random.fold_in(own, position), (parts,), jnp.float32, low / len(split), high / len(split)))
        factor_of = factor_of * jnp.repeat(draws, dims[position] // parts).reshape([-1 if axis == position else 1 for axis in range(len(dims))])
    return factor_of


def scatter_about(key, dims, spread, reach, pieces=(), kind=jnp.bfloat16):
    array = spread * jax.random.normal(key, dims, jnp.float32)
    if pieces:
        array = array * shard_levels(key, dims, pieces, -0.22, 0.18)
    return jnp.clip(array, -reach, reach).astype(kind)


def setup_inputs(seed: int = 0) -> dict:
    splits = jax.random.split(jax.random.key(seed), 4)
    return {
        "momentum_prev": draw_momentum_prev(jax.random.fold_in(splits[3], 71), 0),
        "gradient": scatter_about(splits[1], (D, D), 1.0, 6.0, ((0, 4), (1, 8))),
        "q_prev": scatter_about(splits[2], (D, RANK), D ** -0.5, 0.0625, ((0, 8),), jnp.float32),
    }


def reference(momentum_prev, gradient, q_prev):
    highest = lax.Precision.HIGHEST
    momentum = 0.95 * momentum_prev + gradient.astype(jnp.float32)
    power = jnp.dot(momentum.astype(jnp.float32), q_prev.astype(jnp.float32), precision=highest, preferred_element_type=jnp.float32)
    gram = jnp.dot(power.T.astype(jnp.float32), power.astype(jnp.float32), precision=highest, preferred_element_type=jnp.float32)
    chol = jnp.linalg.cholesky(gram)
    basis = lax.linalg.triangular_solve(chol, power, left_side=False, lower=True, transpose_a=True)
    cross = jnp.dot(momentum.T.astype(jnp.float32), basis.astype(jnp.float32), precision=highest, preferred_element_type=jnp.float32)
    momentum_next = momentum - 0.5 * jnp.dot(basis.astype(jnp.float32), cross.T.astype(jnp.float32), precision=highest, preferred_element_type=jnp.float32)
    col_sq = lax.optimization_barrier(jnp.sum(cross * cross, axis=0))
    q_next = cross / (jnp.sqrt(col_sq) + 1e-08)
    factor = D / jnp.sqrt(jnp.float32(RANK))
    update = (factor * jnp.dot(basis.astype(jnp.float32), q_next.T.astype(jnp.float32), precision=highest, preferred_element_type=jnp.float32)).astype(jnp.bfloat16)
    return (momentum_next, q_next, update)
```

```python
import functools

import jax
import jax.numpy as jnp
from jax import lax
from jax.experimental import pallas as pl
from jax.experimental.pallas import tpu as pltpu
from jax.sharding import PartitionSpec as P

CHUNK = 128
PANEL = 8
F32, BF16 = jnp.float32, jnp.bfloat16
HIGHEST = lax.Precision.HIGHEST
NN = (((1,), (0,)), ((), ()))
NT = (((1,), (1,)), ((), ()))
VMEM_LIMIT = 50 * 1024 * 1024


def params():
    return pltpu.CompilerParams(vmem_limit_bytes=VMEM_LIMIT)


def cost(flops, nbytes):
    return pl.CostEstimate(flops=int(flops), bytes_accessed=int(nbytes), transcendentals=0)


def split(x):
    hi = x.astype(BF16)
    return hi, (x - hi.astype(F32)).astype(BF16)


def dot1(a, b, dims):
    return lax.dot_general(a, b, dims, preferred_element_type=F32)


def dot_high(a, b, dims):
    return lax.dot_general(a, b, dims, precision=HIGHEST, preferred_element_type=F32)


def bit_orders(bits):
    rest = list(range(1, bits))
    half = (len(rest) + 1) // 2
    return rest, rest[half:] + rest[:half]


def position_masks(bits, parity):
    orders = bit_orders(bits)

    def walk(order):
        masks = [0]
        for bit in reversed(order):
            masks = masks + [m ^ (1 << bit) for m in masks]
        return masks

    return walk(orders[parity]) + [1 ^ m for m in walk(orders[1 - parity])]


def pair_perms(bits):
    orders = bit_orders(bits)
    n = 1 << bits
    return [[(j, j ^ (1 << orders[j & 1][step])) for j in range(n)] for step in range(bits - 1)]


def line_all_reduce(parts, axis, n):
    me = lax.axis_index(axis)
    half = n // 2
    done = []
    for x in parts:
        for s in range(half - 1):
            x = x + lax.ppermute(x, axis, [(s, s + 1), (n - 1 - s, n - 2 - s)])
        x = x + lax.ppermute(x, axis, [(half - 1, half), (half, half - 1)])
        for s in reversed(range(half - 1)):
            r = lax.ppermute(x, axis, [(s + 1, s), (n - 2 - s, n - 1 - s)])
            x = jnp.where((me == s) | (me == n - 1 - s), r, x)
        done.append(x)
    return done


def power_kernel(half, chunks, order_ref, mp_ref, g_ref, q_ref, *refs):
    hi_ref, lo_ref = refs[:2]
    keep, send = refs[2 : 2 + chunks], refs[2 + chunks : 2 + 2 * chunks]
    qhi, qlo = refs[2 + 2 * chunks :]
    t = pl.program_id(0)

    @pl.when(t == 0)
    def _():
        h, l = split(q_ref[...].T)
        qhi[...] = h
        qlo[...] = l

    m = 0.95 * mp_ref[...] + g_ref[...].astype(F32)
    h, l = split(m)
    hi_ref[0] = h
    lo_ref[0] = l
    p = dot1(qhi[...], h, NT) + (dot1(qlo[...], h, NT) + dot1(qhi[...], l, NT))

    @pl.when(t < half)
    def _():
        for c in range(chunks):
            keep[c][0] = p[c * CHUNK : (c + 1) * CHUNK]

    @pl.when(t >= half)
    def _():
        for c in range(chunks):
            send[c][0] = p[c * CHUNK : (c + 1) * CHUNK]


def power_call(order, mp, g, q, blocks, chunks):
    rows, cols = mp.shape
    rank = q.shape[1]
    block, half = rows // blocks, blocks // 2
    grid_spec = pltpu.PrefetchScalarGridSpec(
        num_scalar_prefetch=1,
        grid=(blocks,),
        in_specs=[
            pl.BlockSpec((block, cols), lambda t, o: (o[t], 0)),
            pl.BlockSpec((block, cols), lambda t, o: (o[t], 0)),
            pl.BlockSpec((cols, rank), lambda t, o: (0, 0)),
        ],
        out_specs=[pl.BlockSpec((1, block, cols), lambda t, o: (t, 0, 0))] * 2
        + [pl.BlockSpec((1, CHUNK, block), lambda t, o: (jnp.minimum(t, half - 1), 0, 0))] * chunks
        + [pl.BlockSpec((1, CHUNK, block), lambda t, o: (jnp.maximum(t - half, 0), 0, 0))] * chunks,
        scratch_shapes=[pltpu.VMEM((rank, cols), BF16)] * 2,
    )
    out = pl.pallas_call(
        functools.partial(power_kernel, half, chunks),
        grid_spec=grid_spec,
        out_shape=[jax.ShapeDtypeStruct((blocks, block, cols), BF16)] * 2
        + [jax.ShapeDtypeStruct((half, CHUNK, block), F32)] * (2 * chunks),
        compiler_params=params(),
        cost_estimate=cost(6 * rows * cols * rank, 10 * rows * cols + 4 * rank * (rows + cols)),
        name="power",
    )(order, mp, g, q)
    return out[0], out[1], out[2 : 2 + chunks], out[2 + chunks :]


def raw_kernel(half, pa_ref, pb_ref, hi_ref, lo_ref, top_ref, bot_ref, acc):
    t = pl.program_id(0)

    @pl.when(t == 0)
    def _():
        acc[...] = jnp.zeros_like(acc)

    p = jnp.where(t < half, pa_ref[jnp.minimum(t, half - 1)], pb_ref[jnp.maximum(t - half, 0)])
    ph, plo = split(p)
    both = dot1(jnp.concatenate([ph, plo], axis=0), hi_ref[0], NN)
    acc[...] += both[:CHUNK] + (both[CHUNK:] + dot1(ph, lo_ref[0], NN))

    @pl.when(t == 2 * half - 1)
    def _():
        top_ref[...] = acc[: CHUNK // 2]
        bot_ref[...] = acc[CHUNK // 2 :]


def raw_call(pa, pb, hi, lo):
    blocks, block, cols = hi.shape
    whole = pl.BlockSpec(pa.shape, lambda t: (0, 0, 0))
    piece = pl.BlockSpec((CHUNK // 2, cols), lambda t: (0, 0))
    return pl.pallas_call(
        functools.partial(raw_kernel, blocks // 2),
        grid=(blocks,),
        in_specs=[whole, whole] + [pl.BlockSpec((1, block, cols), lambda t: (t, 0, 0))] * 2,
        out_specs=[piece, piece],
        out_shape=[jax.ShapeDtypeStruct((CHUNK // 2, cols), F32)] * 2,
        scratch_shapes=[pltpu.VMEM((CHUNK, cols), F32)],
        compiler_params=params(),
        cost_estimate=cost(8 * blocks * block * cols * CHUNK, 4 * blocks * block * cols),
        name="raw",
    )(pa, pb, hi, lo)


def gram_kernel(half, c, me_ref, *refs):
    pieces, out_ref = refs[:-1], refs[-1]
    out_rows = out_ref.shape[0]
    start = pl.multiple_of(me_ref[0] * out_rows, out_rows)
    for d in range(c + 1):
        total = jnp.zeros((out_rows, CHUNK), F32)
        for side in range(2):
            for t in range(half):
                mine = pieces[2 * c + side][t, pl.ds(start, out_rows), :]
                total += dot_high(mine, pieces[2 * d + side][t], NT)
        out_ref[:, d * CHUNK : (d + 1) * CHUNK] = total


def gram_call(me, parts, c):
    refs = [x for pair in parts[: c + 1] for x in pair]
    half, _, block = refs[0].shape
    rows = CHUNK // (2 * half)
    vmem = pl.BlockSpec(memory_space=pltpu.VMEM)
    return pl.pallas_call(
        functools.partial(gram_kernel, half, c),
        in_specs=[pl.BlockSpec(memory_space=pltpu.SMEM)] + [vmem] * len(refs),
        out_specs=vmem,
        out_shape=jax.ShapeDtypeStruct((rows, (c + 1) * CHUNK), F32),
        compiler_params=params(),
        cost_estimate=cost(12 * CHUNK * (c + 1) * CHUNK * 2 * half * block, 8 * len(refs) * half * block * CHUNK),
        name="gram",
    )(me, *refs)


def eliminate(s_ref, w_ref):
    n = s_ref.shape[0]
    row = lax.broadcasted_iota(jnp.int32, (n, n), 0)
    col = lax.broadcasted_iota(jnp.int32, (n, n), 1)
    w_ref[...] = (row == col).astype(F32)
    full = (PANEL, n)
    sub = lax.broadcasted_iota(jnp.int32, full, 0)
    for base in range(0, n, PANEL):
        panel = s_ref[base : base + PANEL, :]
        wpanel = w_ref[base : base + PANEL, :]
        rows = [jnp.broadcast_to(panel[i : i + 1, :], full) for i in range(PANEL)]
        wrows = [jnp.broadcast_to(wpanel[i : i + 1, :], full) for i in range(PANEL)]
        v = {}
        for i in range(PANEL):
            for k in range(i, PANEL):
                v[i, k] = jnp.broadcast_to(rows[i][:, base + k : base + k + 1], full)
        mult, inv = {}, []
        for i in range(PANEL):
            r = 1.0 / v[i, i]
            inv.append(r)
            for a in range(i + 1, PANEL):
                m = v[i, a] * r
                mult[i, a] = m
                for k in range(a, PANEL):
                    v[a, k] = v[a, k] - m * v[i, k]
                rows[a] = rows[a] - m * rows[i]
                wrows[a] = wrows[a] - m * wrows[i]
        out = wrows[0] * lax.rsqrt(v[0, 0])
        for i in range(1, PANEL):
            out = jnp.where(sub == i, wrows[i] * lax.rsqrt(v[i, i]), out)
        w_ref[base : base + PANEL, :] = out
        for below in range(base + PANEL, n, PANEL):
            s = s_ref[below : below + PANEL, :]
            w = w_ref[below : below + PANEL, :]
            f = [jnp.broadcast_to(s[:, base + i : base + i + 1], full) for i in range(PANEL)]
            for i in range(PANEL):
                for a in range(i + 1, PANEL):
                    f[a] = f[a] - mult[i, a] * f[i]
            for i in range(PANEL):
                g = f[i] * inv[i]
                s = s - g * rows[i]
                w = w - g * wrows[i]
            s_ref[below : below + PANEL, :] = s
            w_ref[below : below + PANEL, :] = w


def chol_kernel(c, n, order_ref, *refs):
    pieces = refs[:n]
    prev = refs[n] if c else None
    out_ref, g_ref, s_ref, w_ref = refs[n + (1 if c else 0) :]
    rows = pieces[0].shape[0]
    for i, piece in enumerate(pieces):
        g_ref[pl.ds(pl.multiple_of(order_ref[i] * rows, rows), rows), :] = piece[...]
    if c:
        left = g_ref[:, : c * CHUNK]
        lrow = dot_high(left, prev[...], NT)
        s_ref[...] = g_ref[:, c * CHUNK :] - dot_high(lrow, lrow, NT)
    else:
        s_ref[...] = g_ref[...]
    eliminate(s_ref, w_ref)
    if c:
        w = w_ref[...]
        out_ref[: c * CHUNK, : c * CHUNK] = prev[...]
        out_ref[: c * CHUNK, c * CHUNK :] = jnp.zeros((c * CHUNK, CHUNK), F32)
        out_ref[c * CHUNK :, : c * CHUNK] = -dot_high(w, dot_high(lrow, prev[...], NN), NN)
        out_ref[c * CHUNK :, c * CHUNK :] = w
    else:
        out_ref[...] = w_ref[...]


def chol_call(order, pieces, prev, c):
    size = (c + 1) * CHUNK
    vmem = pl.BlockSpec(memory_space=pltpu.VMEM)
    args = list(pieces) + ([prev] if c else [])
    return pl.pallas_call(
        functools.partial(chol_kernel, c, len(pieces)),
        in_specs=[pl.BlockSpec(memory_space=pltpu.SMEM)] + [vmem] * len(args),
        out_specs=vmem,
        out_shape=jax.ShapeDtypeStruct((size, size), F32),
        scratch_shapes=[pltpu.VMEM((CHUNK, size), F32), pltpu.VMEM((CHUNK, CHUNK), F32), pltpu.VMEM((CHUNK, CHUNK), F32)],
        compiler_params=params(),
        cost_estimate=cost(6e9, 8 * size * size),
        name="chol",
    )(order, *args)


def basis_kernel(chunks, inv_ref, *refs):
    parts, out_ref, pt = refs[:chunks], refs[chunks], refs[chunks + 1]
    for c in range(chunks):
        pt[c * CHUNK : (c + 1) * CHUNK] = parts[c][0]
    ih, il = split(inv_ref[...])
    ph, plo = split(pt[...])
    out_ref[0] = (dot1(ih, ph, NN) + (dot1(il, ph, NN) + dot1(ih, plo, NN))).T


def basis_call(inv, parts):
    half, _, block = parts[0].shape
    rank = inv.shape[0]
    chunks = len(parts)
    return pl.pallas_call(
        functools.partial(basis_kernel, chunks),
        grid=(half,),
        in_specs=[pl.BlockSpec((rank, rank), lambda t: (0, 0))]
        + [pl.BlockSpec((1, CHUNK, block), lambda t: (t, 0, 0))] * chunks,
        out_specs=pl.BlockSpec((1, block, rank), lambda t: (t, 0, 0)),
        out_shape=jax.ShapeDtypeStruct((half, block, rank), F32),
        scratch_shapes=[pltpu.VMEM((rank, block), F32)],
        compiler_params=params(),
        cost_estimate=cost(6 * rank * rank * block * half, 8 * rank * block * half),
        name="basis",
    )(inv, *parts)


def cross_kernel(n, inv_ref, *refs):
    raws, out_ref, sq_ref = refs[:n], refs[n], refs[n + 1]
    raw = jnp.concatenate([r[...] for r in raws], axis=0)
    ih, il = split(inv_ref[...])
    rh, rl = split(raw)
    cross = dot1(ih, rh, NN) + (dot1(il, rh, NN) + dot1(ih, rl, NN))
    out_ref[...] = cross
    sq_ref[...] = jnp.sum(cross * cross, axis=1, keepdims=True).T


def cross_call(inv, raws):
    rank = inv.shape[0]
    cols = raws[0].shape[1]
    vmem = pl.BlockSpec(memory_space=pltpu.VMEM)
    return pl.pallas_call(
        functools.partial(cross_kernel, len(raws)),
        in_specs=[vmem] * (1 + len(raws)),
        out_specs=[vmem, vmem],
        out_shape=[jax.ShapeDtypeStruct((rank, cols), F32), jax.ShapeDtypeStruct((1, rank), F32)],
        compiler_params=params(),
        cost_estimate=cost(6 * rank * rank * cols, 8 * rank * cols),
        name="cross",
    )(inv, *raws)


def momentum_kernel(half, order_ref, ba_ref, bb_ref, c_ref, hi_ref, lo_ref, out_ref, ch, cl):
    t = pl.program_id(0)

    @pl.when(t == 0)
    def _():
        h, l = split(c_ref[...])
        ch[...] = h
        cl[...] = l

    b = jnp.where(t < half, ba_ref[0], bb_ref[0])
    bh, bl = split(b)
    prod = dot1(bh, ch[...], NN) + (dot1(bl, ch[...], NN) + dot1(bh, cl[...], NN))
    out_ref[...] = (hi_ref[0].astype(F32) + lo_ref[0].astype(F32)) - 0.5 * prod


def update_kernel(half, factor, order_ref, ba_ref, bb_ref, c_ref, sq_ref, out_ref, qn_ref, ch, cl):
    t = pl.program_id(0)

    @pl.when(t == 0)
    def _():
        scale = 1.0 / (jnp.sqrt(sq_ref[...]) + 1e-08)
        q = c_ref[...].T * scale
        qn_ref[...] = q
        h, l = split(q)
        ch[...] = h
        cl[...] = l

    b = jnp.where(t < half, ba_ref[0], bb_ref[0])
    bh, bl = split(b)
    prod = dot1(bh, ch[...], NT) + (dot1(bl, ch[...], NT) + dot1(bh, cl[...], NT))
    out_ref[...] = (factor * prod).astype(BF16)


def last_call(order, ba, bb, cross, extra, momentum):
    half, block, rank = ba.shape
    cols = cross.shape[1]
    blocks = 2 * half
    basis = [
        pl.BlockSpec((1, block, rank), lambda t, o: (jnp.minimum(t, half - 1), 0, 0)),
        pl.BlockSpec((1, block, rank), lambda t, o: (jnp.maximum(t - half, 0), 0, 0)),
    ]
    natural = pl.BlockSpec((block, cols), lambda t, o: (o[t], 0))
    whole = pl.BlockSpec((rank, cols), lambda t, o: (0, 0))
    if momentum:
        kernel, scratch = functools.partial(momentum_kernel, half), (rank, cols)
        more = [pl.BlockSpec((1, block, cols), lambda t, o: (t, 0, 0))] * 2
        out_specs, out_shape = natural, jax.ShapeDtypeStruct((blocks * block, cols), F32)
    else:
        factor = float((extra[1]) / (rank**0.5))
        extra = extra[:1]
        kernel, scratch = functools.partial(update_kernel, half, factor), (cols, rank)
        more = [pl.BlockSpec((1, rank), lambda t, o: (0, 0))]
        out_specs = [natural, pl.BlockSpec((cols, rank), lambda t, o: (0, 0))]
        out_shape = [jax.ShapeDtypeStruct((blocks * block, cols), BF16), jax.ShapeDtypeStruct((cols, rank), F32)]
    return pl.pallas_call(
        kernel,
        grid_spec=pltpu.PrefetchScalarGridSpec(
            num_scalar_prefetch=1,
            grid=(blocks,),
            in_specs=basis + [whole] + more,
            out_specs=out_specs,
            scratch_shapes=[pltpu.VMEM(scratch, BF16)] * 2,
        ),
        out_shape=out_shape,
        compiler_params=params(),
        cost_estimate=cost(6 * blocks * block * cols * rank, 8 * blocks * block * cols),
        name="momentum_next" if momentum else "update",
    )(order, ba, bb, cross, *extra)


def fast(n_rows, n_cols, momentum_prev, gradient, q_prev):
    rank = q_prev.shape[1]
    chunks, bits = rank // CHUNK, n_cols.bit_length() - 1
    me = lax.axis_index("cols")
    masks = jnp.where(
        me % 2 == 0,
        jnp.array(position_masks(bits, 0), jnp.int32),
        jnp.array(position_masks(bits, 1), jnp.int32),
    )
    order = me.astype(jnp.int32) ^ masks
    core = [(j, j ^ 1) for j in range(n_cols)]
    perms = pair_perms(bits)

    hi, lo, keep, send = power_call(order, momentum_prev, gradient, q_prev, n_cols, chunks)
    me1 = me.astype(jnp.int32).reshape(1)
    order_x = me.astype(jnp.int32) ^ jnp.arange(n_cols, dtype=jnp.int32)
    parts, raws, inv = [], [], None
    for c in range(chunks):
        k, r = keep[c], lax.ppermute(send[c], "cols", core)
        for perm in perms:
            n = k.shape[0] // 2
            s = lax.ppermute(k[n:] + r[n:], "cols", perm)
            k, r = k[:n] + r[:n], s
        x = k + r
        for perm in reversed(perms):
            x = jnp.concatenate([x, lax.ppermute(x, "cols", perm)], axis=0)
        parts.append((x, lax.ppermute(x, "cols", core)))
        gram = gram_call(me1, parts, c)
        across = [lax.ppermute(gram, "rows", [(i, i ^ m) for i in range(n_rows)]) for m in range(1, n_rows)]
        across = [gram] + across
        while len(across) > 1:
            across = [a + b for a, b in zip(across[::2], across[1::2])]
        gram = across[0]
        pieces = [gram] + [lax.ppermute(gram, "cols", [(j, j ^ m) for j in range(n_cols)]) for m in range(1, n_cols)]
        raws += line_all_reduce(raw_call(*parts[c], hi, lo), "rows", n_rows)
        inv = chol_call(order_x, pieces, inv, c)
    ba = basis_call(inv, [p[0] for p in parts])
    bb = basis_call(inv, [p[1] for p in parts])
    cross, sq = cross_call(inv, raws)
    sqs = [sq]
    for bit in range(bits):
        sqs.append(sqs[-1] + lax.ppermute(sqs[-1], "cols", [(j, j ^ (1 << bit)) for j in range(n_cols)]))
    momentum_next = last_call(order, ba, bb, cross, (hi, lo), True)
    update, q_next = last_call(order, ba, bb, cross, (sqs[-1], momentum_prev.shape[0] * n_rows), False)
    return momentum_next, q_next, update


def plain(n_rows, n_cols, momentum_prev, gradient, q_prev):
    high = lax.Precision.HIGHEST
    dot = functools.partial(lax.dot_general, precision=high, preferred_element_type=F32)
    momentum = 0.95 * momentum_prev + gradient.astype(F32)
    power = lax.psum_scatter(dot(momentum, q_prev, NN), "cols", scatter_dimension=0, tiled=True)
    power = lax.all_gather(power, "cols", axis=0, tiled=True)
    tn = (((0,), (0,)), ((), ()))
    raw, gram = lax.psum((dot(momentum, power, tn), dot(power, power, tn)), "rows")
    chol = jnp.linalg.cholesky(gram)
    solve = functools.partial(lax.linalg.triangular_solve, chol, left_side=False, lower=True, transpose_a=True)
    basis, cross = solve(power), solve(raw)
    q_next = cross / (jnp.sqrt(lax.psum(jnp.sum(cross * cross, axis=0), "cols")) + 1e-08)
    momentum_next = momentum - 0.5 * dot(basis, cross, NT)
    factor = momentum_prev.shape[0] * n_rows / jnp.sqrt(jnp.float32(q_prev.shape[1]))
    return momentum_next, q_next, (factor * dot(basis, q_next, NT)).astype(BF16)


def solution(mesh):
    n_rows, n_cols = mesh.shape["rows"], mesh.shape["cols"]

    def body(momentum_prev, gradient, q_prev):
        rows, cols = momentum_prev.shape
        block = rows // n_cols
        fits = (
            n_rows & (n_rows - 1) == 0
            and n_cols & (n_cols - 1) == 0
            and 4 <= n_cols <= CHUNK // 8
            and block % 128 == 0
            and cols % 128 == 0
            and q_prev.shape[1] % CHUNK == 0
        )
        return (fast if fits else plain)(n_rows, n_cols, momentum_prev, gradient, q_prev)

    in_specs = (P("rows", "cols"), P("rows", "cols"), P("cols", None))
    out_specs = (P("rows", "cols"), P("cols", None), P("rows", "cols"))
    return jax.shard_map(body, mesh=mesh, in_specs=in_specs, out_specs=out_specs, check_vma=False)
```

```python
import functools

import jax
import jax.numpy as jnp
from jax import lax
from jax.experimental import pallas as pl
from jax.experimental.pallas import tpu as pltpu
from jax.sharding import PartitionSpec as P

CHUNK = 128
PANEL = 8
F32, BF16 = jnp.float32, jnp.bfloat16
HIGHEST = lax.Precision.HIGHEST
NN = (((1,), (0,)), ((), ()))
NT = (((1,), (1,)), ((), ()))
MIB = 1024 * 1024
VMEM = pl.BlockSpec(memory_space=pltpu.VMEM)
SMEM = pl.BlockSpec(memory_space=pltpu.SMEM)
HBM = pl.BlockSpec(memory_space=pltpu.HBM)
DMA = pltpu.SemaphoreType.DMA


def params(mib):
    return pltpu.CompilerParams(vmem_limit_bytes=mib * MIB)


def shape(dims, dtype=F32):
    return jax.ShapeDtypeStruct(dims, dtype)


def cost(flops, nbytes):
    return pl.CostEstimate(flops=int(flops), bytes_accessed=int(nbytes), transcendentals=0)


def split(x):
    hi = x.astype(BF16)
    return hi, (x - hi.astype(F32)).astype(BF16)


def dot1(a, b, dims):
    return lax.dot_general(a, b, dims, preferred_element_type=F32)


def dot3(ah, al, bh, bl, dims=NN):
    return dot1(ah, bh, dims) + (dot1(al, bh, dims) + dot1(ah, bl, dims))


def dot_high(a, b, dims):
    return lax.dot_general(a, b, dims, precision=HIGHEST, preferred_element_type=F32)


def bit_orders(bits):
    rest = list(range(1, bits))
    half = (len(rest) + 1) // 2
    return rest, rest[half:] + rest[:half]


def position_masks(bits, parity):
    orders = bit_orders(bits)

    def walk(order):
        masks = [0]
        for bit in reversed(order):
            masks = masks + [m ^ (1 << bit) for m in masks]
        return masks

    return walk(orders[parity]) + [1 ^ m for m in walk(orders[1 - parity])]


def pair_perms(bits):
    orders = bit_orders(bits)
    n = 1 << bits
    return [[(j, j ^ (1 << orders[j & 1][step])) for j in range(n)] for step in range(bits - 1)]


def after(x, token):
    return lax.optimization_barrier((x, token))[0]


def gather_by_pairs(x, n, axis):
    own = [x] + [lax.ppermute(x, axis, [(j, j ^ m) for j in range(n)]) for m in range(2, n, 2)]
    return own, lax.ppermute(jnp.concatenate(own, axis=0), axis, [(j, j ^ 1) for j in range(n)])


def line_all_reduce(parts, axis, n):
    me = lax.axis_index(axis)
    half = n // 2
    done = []
    for x in parts:
        for s in range(half - 1):
            x = x + lax.ppermute(x, axis, [(s, s + 1), (n - 1 - s, n - 2 - s)])
        x = x + lax.ppermute(x, axis, [(half - 1, half), (half, half - 1)])
        for s in reversed(range(half - 1)):
            r = lax.ppermute(x, axis, [(s + 1, s), (n - 2 - s, n - 1 - s)])
            x = jnp.where((me == s) | (me == n - 1 - s), r, x)
        done.append(x)
    return done


def row_copies(order_ref, src, dst, sems, block):
    out = []
    for t in range(dst.shape[0]):
        rows = pl.ds(pl.multiple_of(order_ref[t] * block, block), block)
        out.append(pltpu.make_async_copy(src.at[rows, :], dst.at[t], sems.at[t]))
        out[-1].start()
    return out


def store_parts(p, t, half, widths, keep, send):
    off = 0
    for g, w in enumerate(widths):
        piece = p[:, off : off + w].T
        if t < half:
            keep[g][t] = piece
        else:
            send[g][t - half] = piece
        off += w


def first_kernel(widths, order_ref, mp_ref, g_ref, q_ref, hi_ref, lo_ref, keep_ref, send_ref, mb, gb, qb, sm, sg, sq):
    blocks, block, _ = mb.shape
    width = widths[0]
    q_copy = pltpu.make_async_copy(q_ref, qb, sq)
    q_copy.start()
    g_copies = row_copies(order_ref, g_ref, gb, sg, block)
    m_copies = row_copies(order_ref, mp_ref, mb, sm, block)
    q_copy.wait()
    qh, ql = split(qb[:, :width])
    for t in range(blocks):
        g_copies[t].wait()
        m_copies[t].wait()
        h, l = split(0.95 * mb[t] + gb[t].astype(F32))
        rows = slice(t * block, (t + 1) * block)
        hi_ref[rows, :] = h
        lo_ref[rows, :] = l
        both = dot1(h, jnp.concatenate([qh, ql], axis=1), NN)
        p = both[:, :width] + (both[:, width:] + dot1(l, qh, NN))
        store_parts(p, t, blocks // 2, widths, [keep_ref], [send_ref])


def first_call(order, mp, g, q, width, blocks):
    rows, cols = mp.shape
    block, half = rows // blocks, blocks // 2
    return pl.pallas_call(
        functools.partial(first_kernel, [width]),
        in_specs=[SMEM, HBM, HBM, HBM],
        out_specs=[VMEM] * 4,
        out_shape=[shape((rows, cols), BF16)] * 2 + [shape((half, width, block))] * 2,
        scratch_shapes=[
            pltpu.VMEM((blocks, block, cols), F32),
            pltpu.VMEM((blocks, block, cols), BF16),
            pltpu.VMEM(q.shape, F32),
            DMA((blocks,)),
            DMA((blocks,)),
            DMA,
        ],
        compiler_params=params(32),
        cost_estimate=cost(6 * rows * cols * width, 6 * rows * cols),
        name="momentum_and_power",
    )(order, mp, g, q)


def rest_kernel(widths, first, hi_ref, lo_ref, q_ref, *refs):
    n = len(widths)
    keep, send, (qb, sem) = refs[:n], refs[n : 2 * n], refs[2 * n :]
    half, _, block = keep[0].shape
    copy = pltpu.make_async_copy(q_ref, qb, sem)
    copy.start()
    copy.wait()
    qh, ql = split(qb[:, first:])
    for t in range(2 * half):
        rows = slice(t * block, (t + 1) * block)
        store_parts(dot3(hi_ref[rows, :], lo_ref[rows, :], qh, ql), t, half, widths, keep, send)


def rest_call(hi, lo, q, widths, blocks):
    rows, cols = hi.shape
    block, half = rows // blocks, blocks // 2
    width = sum(widths)
    out = pl.pallas_call(
        functools.partial(rest_kernel, widths, q.shape[1] - width),
        in_specs=[VMEM, VMEM, HBM],
        out_specs=[VMEM] * (2 * len(widths)),
        out_shape=[shape((half, w, block)) for w in widths] * 2,
        scratch_shapes=[pltpu.VMEM(q.shape, F32), DMA],
        compiler_params=params(16),
        cost_estimate=cost(6 * rows * cols * width, 4 * rows * cols),
        name="power",
    )(hi, lo, q)
    return out[: len(widths)], out[len(widths) :]


def raw_kernel(pa_ref, pb_ref, hi_ref, lo_ref, *refs):
    outs, acc = refs[:-1], refs[-1]
    half, width, block = pa_ref.shape
    for t in range(2 * half):
        ph, plo = split(pa_ref[t] if t < half else pb_ref[t - half])
        rows = slice(t * block, (t + 1) * block)
        both = dot1(jnp.concatenate([ph, plo], axis=0), hi_ref[rows, :], NN)
        term = both[:width] + (both[width:] + dot1(ph, lo_ref[rows, :], NN))
        acc[...] = term if t == 0 else acc[...] + term
    off = 0
    for out in outs:
        out[...] = acc[off : off + out.shape[0]]
        off += out.shape[0]


def raw_call(pa, pb, hi, lo, parts):
    rows, cols = hi.shape
    width = pa.shape[1]
    return pl.pallas_call(
        raw_kernel,
        in_specs=[VMEM] * 4,
        out_specs=[VMEM] * len(parts),
        out_shape=[shape((p, cols)) for p in parts],
        scratch_shapes=[pltpu.VMEM((width, cols), F32)],
        compiler_params=params(16),
        cost_estimate=cost(6 * rows * cols * width, 4 * rows * cols),
        name="raw",
    )(pa, pb, hi, lo)


def gram_kernel(skip, me_ref, *refs):
    pieces, out_ref = refs[:-1], refs[-1]
    half = pieces[0].shape[0]
    slice_rows = CHUNK // (2 * half)
    start = me_ref[0] * slice_rows
    groups = list(zip(pieces[::2], pieces[1::2]))
    sums = [None] * len(groups)
    for t in range(2 * half):
        part = [pair[t // half].at[t % half] for pair in groups]
        mine = []
        off = 0
        for ref in part:
            for c in range(0, ref.shape[0], CHUNK):
                if off + c >= skip:
                    mine.append(ref[pl.ds(pl.multiple_of(c + start, slice_rows), slice_rows), :])
            off += ref.shape[0]
        mine = jnp.concatenate(mine, axis=0)
        for d, ref in enumerate(part):
            term = dot_high(ref[...], mine, NT)
            sums[d] = term if sums[d] is None else sums[d] + term
    off = 0
    for s in sums:
        out_ref[:, off : off + s.shape[0]] = s.T
        off += s.shape[0]


def gram_call(me, parts, skip):
    refs = [x for pair in parts for x in pair]
    half, _, block = refs[0].shape
    size = sum(pair[0].shape[1] for pair in parts)
    rows = (size - skip) // (2 * half)
    return pl.pallas_call(
        functools.partial(gram_kernel, skip),
        in_specs=[SMEM] + [VMEM] * len(refs),
        out_specs=VMEM,
        out_shape=shape((rows, size)),
        compiler_params=params(16),
        cost_estimate=cost(4e9, 8 * len(refs) * half * block * CHUNK),
        name="gram",
    )(me, *refs)


def eliminate(s_ref, w_ref):
    n = s_ref.shape[0]
    row = lax.broadcasted_iota(jnp.int32, (n, n), 0)
    col = lax.broadcasted_iota(jnp.int32, (n, n), 1)
    w_ref[...] = (row == col).astype(F32)
    full = (PANEL, n)
    sub = lax.broadcasted_iota(jnp.int32, full, 0)
    for base in range(0, n, PANEL):
        panel = s_ref[base : base + PANEL, :]
        wpanel = w_ref[base : base + PANEL, :]
        rows = [jnp.broadcast_to(panel[i : i + 1, :], full) for i in range(PANEL)]
        wrows = [jnp.broadcast_to(wpanel[i : i + 1, :], full) for i in range(PANEL)]
        v = {}
        for i in range(PANEL):
            for k in range(i, PANEL):
                v[i, k] = jnp.broadcast_to(rows[i][:, base + k : base + k + 1], full)
        mult, inv = {}, []
        for i in range(PANEL):
            r = 1.0 / v[i, i]
            inv.append(r)
            for a in range(i + 1, PANEL):
                m = v[i, a] * r
                mult[i, a] = m
                for k in range(a, PANEL):
                    v[a, k] = v[a, k] - m * v[i, k]
                rows[a] = rows[a] - m * rows[i]
                wrows[a] = wrows[a] - m * wrows[i]
        out = wrows[0] * lax.rsqrt(v[0, 0])
        for i in range(1, PANEL):
            out = jnp.where(sub == i, wrows[i] * lax.rsqrt(v[i, i]), out)
        w_ref[base : base + PANEL, :] = out
        for below in range(base + PANEL, n, PANEL):
            s = s_ref[below : below + PANEL, :]
            w = w_ref[below : below + PANEL, :]
            f = [jnp.broadcast_to(s[:, base + i : base + i + 1], full) for i in range(PANEL)]
            for i in range(PANEL):
                for a in range(i + 1, PANEL):
                    f[a] = f[a] - mult[i, a] * f[i]
            for i in range(PANEL):
                g = f[i] * inv[i]
                s = s - g * rows[i]
                w = w - g * wrows[i]
            s_ref[below : below + PANEL, :] = s
            w_ref[below : below + PANEL, :] = w


def chol_kernel(n_own, skip, order_ref, *refs):
    own, other = refs[:n_own], refs[n_own]
    prev = refs[n_own + 1] if skip else None
    out_ref, g_ref, s_ref, w_ref = refs[n_own + (2 if skip else 1) :]
    size = out_ref.shape[0]
    rows = own[0].shape[0]
    slice_rows = CHUNK // (2 * n_own)
    for i in range(2 * n_own):
        start = order_ref[i] * slice_rows
        for c in range(rows // slice_rows):
            at = c * slice_rows
            if i < n_own:
                piece = own[i][at : at + slice_rows, :]
            else:
                at += (i - n_own) * rows
                piece = other[at : at + slice_rows, :]
            g_ref[pl.ds(pl.multiple_of(c * CHUNK + start, slice_rows), slice_rows), :] = piece
    if skip:
        out_ref[:skip, :skip] = prev[...]
    for base in range(skip, size, CHUNK):
        here = slice(base, base + CHUNK)
        grow = slice(base - skip, base - skip + CHUNK)
        s = g_ref[grow, here]
        if base:
            before = out_ref[:base, :base]
            lrow = dot_high(g_ref[grow, :base], before, NT)
            s = s - dot_high(lrow, lrow, NT)
        s_ref[...] = s
        eliminate(s_ref, w_ref)
        w = w_ref[...]
        out_ref[here, here] = w
        if base:
            out_ref[:base, here] = jnp.zeros((base, CHUNK), F32)
            out_ref[here, :base] = -dot_high(w, dot_high(lrow, before, NN), NN)


def chol_call(order, own, other, prev, skip):
    size = own[0].shape[1]
    args = list(own) + [other] + ([prev] if skip else [])
    return pl.pallas_call(
        functools.partial(chol_kernel, len(own), skip),
        in_specs=[SMEM] + [VMEM] * len(args),
        out_specs=VMEM,
        out_shape=shape((size, size)),
        scratch_shapes=[pltpu.VMEM((size - skip, size), F32)] + [pltpu.VMEM((CHUNK, CHUNK), F32)] * 2,
        compiler_params=params(16),
        cost_estimate=cost(6e9 * (size - skip) / CHUNK, 8 * size * size),
        name="chol",
    )(order, *args)


def basis_kernel(inv_ref, *refs):
    pieces, (bh_ref, bl_ref) = refs[:-2], refs[-2:]
    half, _, block = pieces[0].shape
    ih, il = split(inv_ref[...])
    for t in range(2 * half):
        pt = jnp.concatenate([p[t % half] for p in pieces[t // half :: 2]], axis=0)
        ph, plo = split(pt)
        rows = slice(t * block, (t + 1) * block)
        bh_ref[rows, :], bl_ref[rows, :] = split(dot3(ih, il, ph, plo).T)


def basis_call(inv, parts):
    refs = [x for pair in parts for x in pair]
    half, _, block = refs[0].shape
    rank = inv.shape[0]
    return pl.pallas_call(
        basis_kernel,
        in_specs=[VMEM] * (1 + len(refs)),
        out_specs=[VMEM, VMEM],
        out_shape=[shape((2 * half * block, rank), BF16)] * 2,
        compiler_params=params(16),
        cost_estimate=cost(12 * rank * rank * block * half, 16 * rank * block * half),
        name="basis",
    )(inv, *refs)


def cross_kernel(skip, inv_ref, *refs):
    raws, (out_ref, ch_ref, cl_ref, sq_ref) = refs[:-4], refs[-4:]
    size = skip + out_ref.shape[0]
    ih, il = split(inv_ref[skip:size, :size])
    rh, rl = split(jnp.concatenate([r[...] for r in raws], axis=0))
    cross = dot3(ih, il, rh, rl)
    out_ref[...] = cross
    ch_ref[...], cl_ref[...] = split(cross)
    sq_ref[...] = jnp.sum(cross * cross, axis=1, keepdims=True).T


def cross_call(inv, raws, skip):
    cols = raws[0].shape[1]
    rows = sum(r.shape[0] for r in raws) - skip
    return pl.pallas_call(
        functools.partial(cross_kernel, skip),
        in_specs=[VMEM] * (1 + len(raws)),
        out_specs=[VMEM] * 4,
        out_shape=[shape((rows, cols)), shape((rows, cols), BF16), shape((rows, cols), BF16), shape((1, rows))],
        compiler_params=params(16),
        cost_estimate=cost(6 * rows * (rows + skip) * cols, 8 * rows * cols),
        name="cross",
    )(inv, *raws)


def store_rows(order_ref, t, buf, out_ref, sem):
    block = buf.shape[1]
    rows = pl.ds(pl.multiple_of(order_ref[t] * block, block), block)
    copy = pltpu.make_async_copy(buf.at[t], out_ref.at[rows, :], sem.at[t])
    copy.start()
    return copy


def momentum_kernel(n, order_ref, bh_ref, bl_ref, hi_ref, lo_ref, *refs):
    ch_refs, cl_refs, (out_ref, ch, cl, buf, sem) = refs[:n], refs[n : 2 * n], refs[2 * n :]
    blocks, block, _ = buf.shape
    off = 0
    for a, b in zip(ch_refs, cl_refs):
        ch[off : off + a.shape[0], :] = a[...]
        cl[off : off + a.shape[0], :] = b[...]
        off += a.shape[0]
    copies = []
    for t in range(blocks):
        rows = slice(t * block, (t + 1) * block)
        prod = dot3(bh_ref[rows, :], bl_ref[rows, :], ch[...], cl[...])
        buf[t] = (hi_ref[rows, :].astype(F32) + lo_ref[rows, :].astype(F32)) - 0.5 * prod
        copies.append(store_rows(order_ref, t, buf, out_ref, sem))
    for copy in copies:
        copy.wait()


def momentum_call(order, bh, bl, hi, lo, chs, cls):
    rows, cols = hi.shape
    rank, blocks = bh.shape[1], order.shape[0]
    return pl.pallas_call(
        functools.partial(momentum_kernel, len(chs)),
        in_specs=[SMEM] + [VMEM] * (4 + 2 * len(chs)),
        out_specs=HBM,
        out_shape=shape((rows, cols)),
        scratch_shapes=[pltpu.VMEM((rank, cols), BF16)] * 2 + [pltpu.VMEM((blocks, rows // blocks, cols), F32), DMA((blocks,))],
        compiler_params=params(16),
        cost_estimate=cost(6 * rows * cols * rank, 8 * rows * cols),
        name="momentum_next",
    )(order, bh, bl, hi, lo, *chs, *cls)


def update_kernel(n, factor, order_ref, bh_ref, bl_ref, *refs):
    crosses, sqs = refs[:n], refs[n : 2 * n]
    out_ref, qn_ref, ch, cl, qt, buf, qbuf, sem, qsem = refs[2 * n :]
    blocks, block, cols = buf.shape
    off = 0
    for c, sq in zip(crosses, sqs):
        size = c.shape[0]
        scale = jnp.broadcast_to(1.0 / (jnp.sqrt(sq[...]) + 1e-08), (CHUNK, size)).T[:, :1]
        q = c[...] * scale
        qt[off : off + size, :] = q
        ch[off : off + size, :], cl[off : off + size, :] = split(q)
        off += size
    copies = []
    step = cols // blocks
    for t in range(blocks):
        rows = slice(t * block, (t + 1) * block)
        prod = dot3(bh_ref[rows, :], bl_ref[rows, :], ch[...], cl[...])
        buf[t] = (factor * prod).astype(BF16)
        copies.append(store_rows(order_ref, t, buf, out_ref, sem))
        qbuf[t] = qt[:, t * step : (t + 1) * step].T
        copy = pltpu.make_async_copy(qbuf.at[t], qn_ref.at[pl.ds(t * step, step), :], qsem.at[t])
        copy.start()
        copies.append(copy)
    for copy in copies:
        copy.wait()


def update_call(order, bh, bl, crosses, sqs, factor):
    rows, rank = bh.shape
    cols, blocks = crosses[0].shape[1], order.shape[0]
    return pl.pallas_call(
        functools.partial(update_kernel, len(crosses), factor),
        in_specs=[SMEM] + [VMEM] * (2 + 2 * len(crosses)),
        out_specs=[HBM, HBM],
        out_shape=[shape((rows, cols), BF16), shape((cols, rank))],
        scratch_shapes=[pltpu.VMEM((rank, cols), BF16)] * 2
        + [
            pltpu.VMEM((rank, cols), F32),
            pltpu.VMEM((blocks, rows // blocks, cols), BF16),
            pltpu.VMEM((blocks, cols // blocks, rank), F32),
            DMA((blocks,)),
            DMA((blocks,)),
        ],
        compiler_params=params(16),
        cost_estimate=cost(6 * rows * cols * rank, 8 * rows * cols),
        name="update",
    )(order, bh, bl, *crosses, *sqs)


def plan(chunks):
    if chunks < 4:
        return [CHUNK] * chunks, [[CHUNK]] * chunks, [chunks - 1]
    last = (chunks - 2) * CHUNK
    groups = [CHUNK, CHUNK, last]
    return groups, [[CHUNK], [CHUNK], [last - CHUNK, CHUNK // 2, CHUNK // 2]], [1, 2]


def fast(n_rows, n_cols, momentum_prev, gradient, q_prev):
    rank = q_prev.shape[1]
    widths, line_parts, ends = plan(rank // CHUNK)
    bits = n_cols.bit_length() - 1
    me = lax.axis_index("cols").astype(jnp.int32)
    masks = jnp.where(
        me % 2 == 0,
        jnp.array(position_masks(bits, 0), jnp.int32),
        jnp.array(position_masks(bits, 1), jnp.int32),
    )
    order = me ^ masks
    parity_order = me ^ jnp.array(list(range(0, n_cols, 2)) + list(range(1, n_cols, 2)), jnp.int32)
    core = [(j, j ^ 1) for j in range(n_cols)]
    perms = pair_perms(bits)

    hi, lo, keep, send = first_call(order, momentum_prev, gradient, q_prev, widths[0], n_cols)
    keep, send = [keep], [send]
    if len(widths) > 1:
        k, s = rest_call(hi, lo, q_prev, widths[1:], n_cols)
        keep, send = keep + list(k), send + list(s)
    parts, raws, inv, skip, crosses = [], [], None, 0, []
    token = None
    for g, width in enumerate(widths):
        k, r = keep[g], lax.ppermute(send[g], "cols", core)
        if token is not None:
            r = after(r, token)
        for perm in perms:
            n = k.shape[0] // 2
            s = lax.ppermute(k[n:] + r[n:], "cols", perm)
            k, r = k[:n] + r[:n], s
        x = token = k + r
        for perm in reversed(perms):
            x = jnp.concatenate([x, lax.ppermute(x, "cols", perm)], axis=0)
        parts.append((x, lax.ppermute(x, "cols", core)))
    done = 0
    for end in ends:
        gram = gram_call(me.reshape(1), parts[: end + 1], skip)
        across = [gram] + [lax.ppermute(gram, "rows", [(i, i ^ m) for i in range(n_rows)]) for m in range(1, n_rows)]
        while len(across) > 1:
            across = [a + b for a, b in zip(across[::2], across[1::2])]
        own, other = gather_by_pairs(across[0], n_cols, "cols")
        inv = chol_call(parity_order, own, other, inv, skip)
        for g in range(done, end + 1):
            raws += line_all_reduce(raw_call(*parts[g], hi, lo, line_parts[g]), "rows", n_rows)
        crosses.append(cross_call(inv, raws, skip))
        skip, done = sum(widths[: end + 1]), end + 1
    bh, bl = basis_call(inv, parts)
    sqs = []
    for c in crosses:
        own, other = gather_by_pairs(c[3], n_cols, "cols")
        sqs.append(sum(own[1:], own[0]) + jnp.sum(other, axis=0, keepdims=True))
    momentum_next = momentum_call(order, bh, bl, hi, lo, [c[1] for c in crosses], [c[2] for c in crosses])
    factor = momentum_prev.shape[0] * n_rows / rank**0.5
    update, q_next = update_call(order, bh, bl, [c[0] for c in crosses], sqs, factor)
    return momentum_next, q_next, update


def plain(n_rows, n_cols, momentum_prev, gradient, q_prev):
    high = lax.Precision.HIGHEST
    dot = functools.partial(lax.dot_general, precision=high, preferred_element_type=F32)
    momentum = 0.95 * momentum_prev + gradient.astype(F32)
    power = lax.psum_scatter(dot(momentum, q_prev, NN), "cols", scatter_dimension=0, tiled=True)
    power = lax.all_gather(power, "cols", axis=0, tiled=True)
    tn = (((0,), (0,)), ((), ()))
    raw, gram = lax.psum((dot(momentum, power, tn), dot(power, power, tn)), "rows")
    chol = jnp.linalg.cholesky(gram)
    solve = functools.partial(lax.linalg.triangular_solve, chol, left_side=False, lower=True, transpose_a=True)
    basis, cross = solve(power), solve(raw)
    q_next = cross / (jnp.sqrt(lax.psum(jnp.sum(cross * cross, axis=0), "cols")) + 1e-08)
    momentum_next = momentum - 0.5 * dot(basis, cross, NT)
    factor = momentum_prev.shape[0] * n_rows / jnp.sqrt(jnp.float32(q_prev.shape[1]))
    return momentum_next, q_next, (factor * dot(basis, q_next, NT)).astype(BF16)


def solution(mesh):
    n_rows, n_cols = mesh.shape["rows"], mesh.shape["cols"]

    def body(momentum_prev, gradient, q_prev):
        rows, cols = momentum_prev.shape
        block = rows // n_cols
        fits = (
            n_rows & (n_rows - 1) == 0
            and n_cols & (n_cols - 1) == 0
            and 4 <= n_cols <= CHUNK // 8
            and block % 128 == 0
            and cols % 128 == 0
            and q_prev.shape[1] % CHUNK == 0
        )
        return (fast if fits else plain)(n_rows, n_cols, momentum_prev, gradient, q_prev)

    in_specs = (P("rows", "cols"), P("rows", "cols"), P("cols", None))
    out_specs = (P("rows", "cols"), P("cols", None), P("rows", "cols"))
    return jax.shard_map(body, mesh=mesh, in_specs=in_specs, out_specs=out_specs, check_vma=False)
```

```python
import functools

import jax
import jax.numpy as jnp
from jax import lax
from jax.experimental import pallas as pl
from jax.experimental.pallas import tpu as pltpu
from jax.sharding import PartitionSpec as P

CHUNK = 128
SHRINK = 1
PANEL = 8
F32, BF16 = jnp.float32, jnp.bfloat16
HIGHEST = lax.Precision.HIGHEST
NN = (((1,), (0,)), ((), ()))
NT = (((1,), (1,)), ((), ()))
MIB = 1024 * 1024
VMEM = pl.BlockSpec(memory_space=pltpu.VMEM)
SMEM = pl.BlockSpec(memory_space=pltpu.SMEM)
HBM = pl.BlockSpec(memory_space=pltpu.HBM)
DMA = pltpu.SemaphoreType.DMA


def params(mib):
    return pltpu.CompilerParams(vmem_limit_bytes=mib * MIB)


def shape(dims, dtype=F32):
    return jax.ShapeDtypeStruct(dims, dtype)


def cost(flops, nbytes):
    return pl.CostEstimate(flops=int(flops) // SHRINK, bytes_accessed=int(nbytes) // SHRINK, transcendentals=0)


def split(x):
    hi = x.astype(BF16)
    return hi, (x - hi.astype(F32)).astype(BF16)


def dot1(a, b, dims):
    return lax.dot_general(a, b, dims, preferred_element_type=F32)


def dot3(ah, al, bh, bl, dims=NN):
    return dot1(ah, bh, dims) + (dot1(al, bh, dims) + dot1(ah, bl, dims))


def dot_high(a, b, dims):
    return lax.dot_general(a, b, dims, precision=HIGHEST, preferred_element_type=F32)


def bit_orders(bits):
    rest = list(range(1, bits))
    half = (len(rest) + 1) // 2
    return rest, rest[half:] + rest[:half]


def position_masks(bits, parity):
    orders = bit_orders(bits)

    def walk(order):
        masks = [0]
        for bit in reversed(order):
            masks = masks + [m ^ (1 << bit) for m in masks]
        return masks

    return walk(orders[parity]) + [1 ^ m for m in walk(orders[1 - parity])]


def pair_perms(bits):
    orders = bit_orders(bits)
    n = 1 << bits
    return [[(j, j ^ (1 << orders[j & 1][step])) for j in range(n)] for step in range(bits - 1)]


class Order:
    def __init__(self):
        self.token = None

    def __call__(self, f, *args):
        if self.token is not None:
            args, _ = lax.optimization_barrier((args, self.token))
        out = f(*args)
        self.token = jax.tree.leaves(out)[0]
        return out


def in_hbm(*xs):
    return [pltpu.with_memory_space_constraint(x, pltpu.HBM) for x in xs]


def in_vmem(*xs):
    return [pltpu.with_memory_space_constraint(x, pltpu.VMEM) for x in xs]


class Sent:
    def __init__(self, then, stages, x):
        self.then, self.stages = then, list(stages)
        self.send(x)

    def send(self, x):
        self.x = x
        if self.stages:
            self.received = lax.ppermute(x, *self.stages[0][1:])

    def step(self):
        combine = self.stages.pop(0)[0]
        self.send(self.then(combine, self.x, self.received))

    def finish(self):
        while self.stages:
            self.step()
        return self.x


def join(x, r):
    return jnp.concatenate([x, r], axis=0)


def xor_stages(combine, axis, n):
    bits = range(n.bit_length() - 1)
    return [(combine, axis, [(i, i ^ (1 << bit)) for i in range(n)]) for bit in bits]


def line_stages(axis, n):
    me, half = lax.axis_index(axis), n // 2
    stages = [(jnp.add, axis, [(s, s + 1), (n - 1 - s, n - 2 - s)]) for s in range(half - 1)]
    stages.append((jnp.add, axis, [(half - 1, half), (half, half - 1)]))
    for s in reversed(range(half - 1)):
        ends = (me == s) | (me == n - 1 - s)
        take = functools.partial(lambda ends, x, r: jnp.where(ends, r, x), ends)
        stages.append((take, axis, [(s + 1, s), (n - 2 - s, n - 1 - s)]))
    return stages


def row_copies(order_ref, pairs, block):
    out = []
    for t in range(pairs[0][1].shape[0]):
        rows = pl.ds(pl.multiple_of(order_ref[t] * block, block), block)
        out.append([pltpu.make_async_copy(src.at[rows, :], dst.at[t], sems.at[t]) for src, dst, sems in pairs])
        for copy in out[-1]:
            copy.start()
    return out


def store_parts(p, t, half, widths, keep, send):
    off = 0
    for g, w in enumerate(widths):
        piece = p[:, off : off + w].T
        if t < half:
            keep[g][t] = piece
        else:
            send[g][t - half] = piece
        off += w


def first_kernel(widths, order_ref, mp_ref, g_ref, q_ref, hi_ref, lo_ref, keep_ref, send_ref, mb, gb, qb, sm, sg, sq):
    blocks, block, _ = mb.shape
    width = widths[0]
    q_copy = pltpu.make_async_copy(q_ref, qb, sq)
    q_copy.start()
    copies = row_copies(order_ref, [(mp_ref, mb, sm), (g_ref, gb, sg)], block)
    q_copy.wait()
    qh, ql = split(qb[:, :width])
    both_q = jnp.concatenate([qh, ql], axis=1)

    def momentum(t):
        for copy in copies[t]:
            copy.wait()
        h, l = split(0.95 * mb[t] + gb[t].astype(F32))
        rows = slice(t * block, (t + 1) * block)
        hi_ref[rows, :] = h
        lo_ref[rows, :] = l
        return h, l

    now = momentum(0)
    for t in range(blocks):
        later = momentum(t + 1) if t + 1 < blocks else None
        h, l = now
        both = dot1(h, both_q, NN)
        p = both[:, :width] + (both[:, width:] + dot1(l, qh, NN))
        store_parts(p, t, blocks // 2, widths, [keep_ref], [send_ref])
        now = later


def first_call(order, mp, g, q, width, blocks):
    rows, cols = mp.shape
    block, half = rows // blocks, blocks // 2
    return pl.pallas_call(
        functools.partial(first_kernel, [width]),
        in_specs=[SMEM, HBM, HBM, HBM],
        out_specs=[VMEM] * 4,
        out_shape=[pltpu.VMEM((rows, cols), BF16)] * 2 + [shape((half, width, block))] * 2,
        scratch_shapes=[
            pltpu.VMEM((blocks, block, cols), F32),
            pltpu.VMEM((blocks, block, cols), BF16),
            pltpu.VMEM(q.shape, F32),
            DMA((blocks,)),
            DMA((blocks,)),
            DMA,
        ],
        compiler_params=params(24),
        cost_estimate=cost(6 * rows * cols * width, 6 * rows * cols),
        name="momentum_and_power",
    )(order, *in_hbm(mp, g, q))


def rest_kernel(widths, first, hi_ref, lo_ref, q_ref, *refs):
    n = len(widths)
    keep, send, (qb, sem) = refs[:n], refs[n : 2 * n], refs[2 * n :]
    half, _, block = keep[0].shape
    copy = pltpu.make_async_copy(q_ref, qb, sem)
    copy.start()
    copy.wait()
    qh, ql = split(qb[:, first:])
    for t in range(2 * half):
        rows = slice(t * block, (t + 1) * block)
        store_parts(dot3(hi_ref[rows, :], lo_ref[rows, :], qh, ql), t, half, widths, keep, send)


def rest_call(hi, lo, q, widths, blocks):
    rows, cols = hi.shape
    block, half = rows // blocks, blocks // 2
    width = sum(widths)
    out = pl.pallas_call(
        functools.partial(rest_kernel, widths, q.shape[1] - width),
        in_specs=[VMEM, VMEM, HBM],
        out_specs=[VMEM] * (2 * len(widths)),
        out_shape=[shape((half, w, block)) for w in widths] * 2,
        scratch_shapes=[pltpu.VMEM(q.shape, F32), DMA],
        compiler_params=params(16),
        cost_estimate=cost(6 * rows * cols * width, 4 * rows * cols),
        name="power",
    )(*in_vmem(hi, lo), *in_hbm(q))
    return out[: len(widths)], out[len(widths) :]


def raw_kernel(pa_ref, pb_ref, hi_ref, lo_ref, *refs):
    outs, acc = refs[:-1], refs[-1]
    half, width, block = pa_ref.shape
    for t in range(2 * half):
        ph, plo = split(pa_ref[t] if t < half else pb_ref[t - half])
        rows = slice(t * block, (t + 1) * block)
        both = dot1(jnp.concatenate([ph, plo], axis=0), hi_ref[rows, :], NN)
        term = both[:width] + (both[width:] + dot1(ph, lo_ref[rows, :], NN))
        acc[...] = term if t == 0 else acc[...] + term
    off = 0
    for out in outs:
        out[...] = acc[off : off + out.shape[0]]
        off += out.shape[0]


def raw_call(pa, pb, hi, lo, parts):
    rows, cols = hi.shape
    width = pa.shape[1]
    return pl.pallas_call(
        raw_kernel,
        in_specs=[VMEM] * 4,
        out_specs=[VMEM] * len(parts),
        out_shape=[shape((p, cols)) for p in parts],
        scratch_shapes=[pltpu.VMEM((width, cols), F32)],
        compiler_params=params(16),
        cost_estimate=cost(6 * rows * cols * width, 4 * rows * cols),
        name="raw",
    )(pa, pb, *in_vmem(hi, lo))


def gram_kernel(skip, me_ref, *refs):
    pieces, out_ref = refs[:-1], refs[-1]
    half = pieces[0].shape[0]
    slice_rows = CHUNK // (2 * half)
    start = me_ref[0] * slice_rows
    groups = list(zip(pieces[::2], pieces[1::2]))
    sums = [None] * len(groups)
    for t in range(2 * half):
        part = [pair[t // half].at[t % half] for pair in groups]
        mine = []
        off = 0
        for ref in part:
            for c in range(0, ref.shape[0], CHUNK):
                if off + c >= skip:
                    mine.append(ref[pl.ds(pl.multiple_of(c + start, slice_rows), slice_rows), :])
            off += ref.shape[0]
        mine = jnp.concatenate(mine, axis=0)
        for d, ref in enumerate(part):
            term = dot_high(ref[...], mine, NT)
            sums[d] = term if sums[d] is None else sums[d] + term
    off = 0
    for s in sums:
        out_ref[:, off : off + s.shape[0]] = s.T
        off += s.shape[0]


def gram_call(me, parts, skip):
    refs = [x for pair in parts for x in pair]
    half, _, block = refs[0].shape
    size = sum(pair[0].shape[1] for pair in parts)
    rows = (size - skip) // (2 * half)
    return pl.pallas_call(
        functools.partial(gram_kernel, skip),
        in_specs=[SMEM] + [VMEM] * len(refs),
        out_specs=VMEM,
        out_shape=shape((rows, size)),
        compiler_params=params(16),
        cost_estimate=cost(4e9, 8 * len(refs) * half * block * CHUNK),
        name="gram",
    )(me, *refs)


def eliminate(s_ref, w_ref):
    n = s_ref.shape[0]
    row = lax.broadcasted_iota(jnp.int32, (n, n), 0)
    col = lax.broadcasted_iota(jnp.int32, (n, n), 1)
    w_ref[...] = (row == col).astype(F32)
    full = (PANEL, n)
    sub = lax.broadcasted_iota(jnp.int32, full, 0)
    for base in range(0, n, PANEL):
        panel = s_ref[base : base + PANEL, :]
        wpanel = w_ref[base : base + PANEL, :]
        rows = [jnp.broadcast_to(panel[i : i + 1, :], full) for i in range(PANEL)]
        wrows = [jnp.broadcast_to(wpanel[i : i + 1, :], full) for i in range(PANEL)]
        v = {}
        for i in range(PANEL):
            for k in range(i, PANEL):
                v[i, k] = jnp.broadcast_to(rows[i][:, base + k : base + k + 1], full)
        mult, inv = {}, []
        for i in range(PANEL):
            r = 1.0 / v[i, i]
            inv.append(r)
            for a in range(i + 1, PANEL):
                m = v[i, a] * r
                mult[i, a] = m
                for k in range(a, PANEL):
                    v[a, k] = v[a, k] - m * v[i, k]
                rows[a] = rows[a] - m * rows[i]
                wrows[a] = wrows[a] - m * wrows[i]
        out = wrows[0] * lax.rsqrt(v[0, 0])
        for i in range(1, PANEL):
            out = jnp.where(sub == i, wrows[i] * lax.rsqrt(v[i, i]), out)
        w_ref[base : base + PANEL, :] = out
        for below in range(base + PANEL, n, PANEL):
            s = s_ref[below : below + PANEL, :]
            w = w_ref[below : below + PANEL, :]
            f = [jnp.broadcast_to(s[:, base + i : base + i + 1], full) for i in range(PANEL)]
            for i in range(PANEL):
                for a in range(i + 1, PANEL):
                    f[a] = f[a] - mult[i, a] * f[i]
            for i in range(PANEL):
                g = f[i] * inv[i]
                s = s - g * rows[i]
                w = w - g * wrows[i]
            s_ref[below : below + PANEL, :] = s
            w_ref[below : below + PANEL, :] = w


def chol_kernel(n, skip, order_ref, gram_ref, *refs):
    prev = refs[0] if skip else None
    out_ref, g_ref, s_ref, w_ref = refs[1 if skip else 0 :]
    size = out_ref.shape[0]
    rows, slice_rows = gram_ref.shape[0] // n, CHUNK // n
    for i in range(n):
        start = order_ref[i] * slice_rows
        for c in range(rows // slice_rows):
            at = i * rows + c * slice_rows
            to = pl.ds(pl.multiple_of(c * CHUNK + start, slice_rows), slice_rows)
            g_ref[to, :] = gram_ref[at : at + slice_rows, :]
    if skip:
        out_ref[:skip, :skip] = prev[...]
    for base in range(skip, size, CHUNK):
        here = slice(base, base + CHUNK)
        grow = slice(base - skip, base - skip + CHUNK)
        s = g_ref[grow, here]
        if base:
            before = out_ref[:base, :base]
            lrow = dot_high(g_ref[grow, :base], before, NT)
            s = s - dot_high(lrow, lrow, NT)
        s_ref[...] = s
        eliminate(s_ref, w_ref)
        w = w_ref[...]
        out_ref[here, here] = w
        if base:
            out_ref[:base, here] = jnp.zeros((base, CHUNK), F32)
            out_ref[here, :base] = -dot_high(w, dot_high(lrow, before, NN), NN)


def chol_call(order, gram, prev, skip):
    size = gram.shape[1]
    args = [gram] + ([prev] if skip else [])
    return pl.pallas_call(
        functools.partial(chol_kernel, order.shape[0], skip),
        in_specs=[SMEM] + [VMEM] * len(args),
        out_specs=VMEM,
        out_shape=shape((size, size)),
        scratch_shapes=[pltpu.VMEM((size - skip, size), F32)] + [pltpu.VMEM((CHUNK, CHUNK), F32)] * 2,
        compiler_params=params(8),
        cost_estimate=cost(6e9 * (size - skip) / CHUNK, 8 * size * size),
        name="chol",
    )(order, *args)


def basis_kernel(inv_ref, *refs):
    pieces, (bh_ref, bl_ref) = refs[:-2], refs[-2:]
    half, _, block = pieces[0].shape
    ih, il = split(inv_ref[...])
    for t in range(2 * half):
        pt = jnp.concatenate([p[t % half] for p in pieces[t // half :: 2]], axis=0)
        ph, plo = split(pt)
        rows = slice(t * block, (t + 1) * block)
        bh_ref[rows, :], bl_ref[rows, :] = split(dot3(ih, il, ph, plo).T)


def basis_call(inv, parts):
    refs = [x for pair in parts for x in pair]
    half, _, block = refs[0].shape
    rank = inv.shape[0]
    return pl.pallas_call(
        basis_kernel,
        in_specs=[VMEM] * (1 + len(refs)),
        out_specs=[VMEM, VMEM],
        out_shape=[pltpu.VMEM((2 * half * block, rank), BF16)] * 2,
        compiler_params=params(16),
        cost_estimate=cost(12 * rank * rank * block * half, 16 * rank * block * half),
        name="basis",
    )(inv, *refs)


def cross_kernel(skip, inv_ref, *refs):
    raws, (out_ref, ch_ref, cl_ref, sq_ref) = refs[:-4], refs[-4:]
    size = skip + out_ref.shape[0]
    ih, il = split(inv_ref[skip:size, :size])
    rh, rl = split(jnp.concatenate([r[...] for r in raws], axis=0))
    cross = dot3(ih, il, rh, rl)
    out_ref[...] = cross
    ch_ref[...], cl_ref[...] = split(cross)
    sq_ref[...] = jnp.sum(cross * cross, axis=1, keepdims=True).T


def cross_call(inv, raws, skip):
    cols = raws[0].shape[1]
    rows = sum(r.shape[0] for r in raws) - skip
    return pl.pallas_call(
        functools.partial(cross_kernel, skip),
        in_specs=[VMEM] * (1 + len(raws)),
        out_specs=[VMEM] * 4,
        out_shape=[pltpu.VMEM((rows, cols), F32), pltpu.VMEM((rows, cols), BF16), pltpu.VMEM((rows, cols), BF16), shape((1, rows))],
        compiler_params=params(16),
        cost_estimate=cost(6 * rows * (rows + skip) * cols, 8 * rows * cols),
        name="cross",
    )(inv, *raws)


def store_rows(order_ref, place, buf, t, out_ref, sem):
    block = buf.shape[1]
    rows = pl.ds(pl.multiple_of(order_ref[place] * block, block), block)
    copy = pltpu.make_async_copy(buf.at[t], out_ref.at[rows, :], sem.at[t])
    copy.start()
    return copy


def momentum_kernel(n, first, order_ref, bh_ref, bl_ref, hi_ref, lo_ref, *refs):
    ch_refs, cl_refs = refs[:n], refs[n : 2 * n]
    out_ref, ch, cl, buf, sem = refs[-5:]
    blocks, block, _ = buf.shape
    off = 0
    for a, b in zip(ch_refs, cl_refs):
        ch[off : off + a.shape[0], :] = a[...]
        cl[off : off + a.shape[0], :] = b[...]
        off += a.shape[0]
    copies = []
    for t in range(blocks):
        rows = slice((first + t) * block, (first + t + 1) * block)
        prod = dot3(bh_ref[rows, :], bl_ref[rows, :], ch[...], cl[...])
        buf[t] = (hi_ref[rows, :].astype(F32) + lo_ref[rows, :].astype(F32)) - 0.5 * prod
        copies.append(store_rows(order_ref, first + t, buf, t, out_ref, sem))
    for copy in copies:
        copy.wait()


def momentum_call(order, bh, bl, hi, lo, chs, cls, first, so_far):
    rows, cols = hi.shape
    rank, blocks = bh.shape[1], order.shape[0]
    more = [] if so_far is None else [so_far]
    args = in_vmem(bh, bl, hi, lo, *chs, *cls)
    return pl.pallas_call(
        functools.partial(momentum_kernel, len(chs), first),
        in_specs=[SMEM] + [VMEM] * len(args) + [HBM] * len(more),
        out_specs=HBM,
        out_shape=shape((rows, cols)),
        scratch_shapes=[pltpu.VMEM((rank, cols), BF16)] * 2
        + [pltpu.VMEM((blocks // 2, rows // blocks, cols), F32), DMA((blocks // 2,))],
        input_output_aliases={1 + len(args): 0} if more else {},
        compiler_params=params(12),
        cost_estimate=cost(3 * rows * cols * rank, 4 * rows * cols),
        name="momentum_next",
    )(order, *args, *more)


def update_kernel(n, factor, order_ref, bh_ref, bl_ref, *refs):
    crosses, sqs = refs[:n], refs[n : 2 * n]
    out_ref, qn_ref, ch, cl, qt, buf, qbuf, sem, qsem = refs[2 * n :]
    blocks, block, cols = buf.shape
    off = 0
    for c, sq in zip(crosses, sqs):
        size = c.shape[0]
        total = jnp.sum(sq[...], axis=0, keepdims=True)
        scale = jnp.broadcast_to(1.0 / (jnp.sqrt(total) + 1e-08), (CHUNK, size)).T[:, :1]
        q = c[...] * scale
        qt[off : off + size, :] = q
        ch[off : off + size, :], cl[off : off + size, :] = split(q)
        off += size
    copies = []
    step = cols // blocks
    for t in range(blocks):
        rows = slice(t * block, (t + 1) * block)
        prod = dot3(bh_ref[rows, :], bl_ref[rows, :], ch[...], cl[...])
        buf[t] = (factor * prod).astype(BF16)
        copies.append(store_rows(order_ref, t, buf, t, out_ref, sem))
        qbuf[t] = qt[:, t * step : (t + 1) * step].T
        copy = pltpu.make_async_copy(qbuf.at[t], qn_ref.at[pl.ds(t * step, step), :], qsem.at[t])
        copy.start()
        copies.append(copy)
    for copy in copies:
        copy.wait()


def update_call(order, bh, bl, crosses, sqs, factor):
    rows, rank = bh.shape
    cols, blocks = crosses[0].shape[1], order.shape[0]
    return pl.pallas_call(
        functools.partial(update_kernel, len(crosses), factor),
        in_specs=[SMEM] + [VMEM] * (2 + 2 * len(crosses)),
        out_specs=[HBM, HBM],
        out_shape=[shape((rows, cols), BF16), shape((cols, rank))],
        scratch_shapes=[pltpu.VMEM((rank, cols), BF16)] * 2
        + [
            pltpu.VMEM((rank, cols), F32),
            pltpu.VMEM((blocks, rows // blocks, cols), BF16),
            pltpu.VMEM((blocks, cols // blocks, rank), F32),
            DMA((blocks,)),
            DMA((blocks,)),
        ],
        compiler_params=params(16),
        cost_estimate=cost(6 * rows * cols * rank, 8 * rows * cols),
        name="update",
    )(order, *in_vmem(bh, bl, *crosses), *sqs)


def fast(n_rows, n_cols, momentum_prev, gradient, q_prev):
    rank = q_prev.shape[1]
    width = rank // 2
    bits = n_cols.bit_length() - 1
    me = lax.axis_index("cols").astype(jnp.int32)
    masks = jnp.where(
        me % 2 == 0,
        jnp.array(position_masks(bits, 0), jnp.int32),
        jnp.array(position_masks(bits, 1), jnp.int32),
    )
    order = me ^ masks
    xor_order = me ^ jnp.arange(n_cols, dtype=jnp.int32)
    core = [(j, j ^ 1) for j in range(n_cols)]
    perms = pair_perms(bits)
    then = Order()

    def halve(k, r):
        n = k.shape[0] // 2
        return k[n:] + r[n:], k[:n] + r[:n]

    def reduce_step(k, r, perm):
        s, k = then(halve, k, r)
        return k, lax.ppermute(s, "cols", perm)

    def gather_step(x, r, perm):
        x = then(join, x, r)
        return x, lax.ppermute(x, "cols", perm)

    gram_stages = xor_stages(jnp.add, "rows", n_rows) + xor_stages(join, "cols", n_cols)
    norm_stages = xor_stages(jnp.add, "cols", n_cols)

    def on_line(pieces):
        return [Sent(then, line_stages("rows", n_rows), then(lambda x: x, p)) for p in pieces]

    hi, lo, keep, send = then(lambda *x: first_call(*x, width, n_cols), order, momentum_prev, gradient, q_prev)
    a, ra = keep, lax.ppermute(send, "cols", core)
    a, ra = reduce_step(a, ra, perms[0])
    (keep,), (send,) = then(lambda h, l, q: rest_call(h, l, q, [width], n_cols), hi, lo, q_prev)
    b, rb = keep, lax.ppermute(send, "cols", core)
    for perm in perms[1:]:
        a, ra = reduce_step(a, ra, perm)
    a = then(jnp.add, a, ra)
    ra = lax.ppermute(a, "cols", perms[-1])
    for perm in reversed(perms[1:-1]):
        a, ra = gather_step(a, ra, perm)

    def both_steps(a, ra, b, rb):
        s, b = halve(b, rb)
        a = join(a, ra)
        return join(a, s), a, b

    s, a, b = then(both_steps, a, ra, b, rb)
    s = lax.ppermute(s, "cols", perms[0])
    n = a.shape[0]
    a = then(lambda a, s: join(a, s[:n]), a, s)
    ra, rb = lax.ppermute(a, "cols", core), s[n:]
    b, rb = reduce_step(b, rb, perms[1])
    pa = (a, ra)
    raw = then(lambda x, y, h, l: raw_call(x, y, h, l, [CHUNK] * (width // CHUNK)), *pa, hi, lo)
    line_a = on_line(raw[:1])
    gram_a = Sent(then, gram_stages, then(lambda m, x, y: gram_call(m, [(x, y)], 0), me.reshape(1), *pa))
    line_a += on_line(raw[1:])
    for perm in perms[2:]:
        b, rb = reduce_step(b, rb, perm)
    b = then(jnp.add, b, rb)
    rb = lax.ppermute(b, "cols", perms[-1])
    gram_a.step()
    for perm in reversed(perms[:-1]):
        b, rb = gather_step(b, rb, perm)
    line_a[0].step()
    gram_a.step()
    b, rb = gather_step(b, rb, core)
    pb = (b, rb)
    gram_a.step()
    gram_b = Sent(then, gram_stages, then(lambda m, *p: gram_call(m, [p[:2], p[2:]], width), me.reshape(1), *pa, *pb))
    small = [CHUNK] * (width // CHUNK - 1) + [CHUNK // 2] * 2
    raw = then(lambda x, y, h, l: raw_call(x, y, h, l, small), *pb, hi, lo)
    gram_b.step()
    line_b = on_line(raw)
    gram_a.step()
    line_a[1].step()
    line_a[0].step()
    gram_b.step()
    gram_a.finish()
    gram_b.step()
    inv = then(lambda o, g: chol_call(o, g, None, 0), xor_order, gram_a.x)
    gram_b.step()
    line_b[0].step()
    line_a[1].step()
    line_a[0].finish()
    gram_b.finish()
    line_b[1].step()
    inv = then(lambda o, g, i: chol_call(o, g, i, width), xor_order, gram_b.x, inv)
    line_b[0].step()
    line_b[2].step()
    line_b[1].step()
    raws = [part.finish() for part in line_a]
    line_b[2].step()
    cross_a = then(lambda i, *r: cross_call(i, r, 0), inv, *raws)
    norm_a = Sent(then, norm_stages, cross_a[3])
    bh, bl = then(lambda i, *p: basis_call(i, [p[:2], p[2:]]), inv, *pa, *pb)
    norm_a.step()
    line_b[0].finish()
    norm_a.step()
    line_b[1].finish()
    norm_a.finish()
    raws += [part.finish() for part in line_b]
    cross_b = then(lambda i, *r: cross_call(i, r, width), inv, *raws)
    norm_b = Sent(then, norm_stages, cross_b[3])
    norm_b.step()
    crosses = [cross_a, cross_b]
    chs, cls = [c[1] for c in crosses], [c[2] for c in crosses]
    part = then(lambda *x: momentum_call(*x, 0, None), order, bh, bl, hi, lo, chs, cls)
    norm_b.step()
    momentum_next = then(lambda p, *x: momentum_call(*x, n_cols // 2, p), part, order, bh, bl, hi, lo, chs, cls)
    norm_b.finish()
    factor = momentum_prev.shape[0] * n_rows / rank**0.5
    sqs = [norm_a.x, norm_b.x]
    update, q_next = then(lambda *x: update_call(*x, factor), order, bh, bl, [c[0] for c in crosses], sqs)
    return momentum_next, q_next, update


def plain(n_rows, n_cols, momentum_prev, gradient, q_prev):
    high = lax.Precision.HIGHEST
    dot = functools.partial(lax.dot_general, precision=high, preferred_element_type=F32)
    momentum = 0.95 * momentum_prev + gradient.astype(F32)
    power = lax.psum_scatter(dot(momentum, q_prev, NN), "cols", scatter_dimension=0, tiled=True)
    power = lax.all_gather(power, "cols", axis=0, tiled=True)
    tn = (((0,), (0,)), ((), ()))
    raw, gram = lax.psum((dot(momentum, power, tn), dot(power, power, tn)), "rows")
    chol = jnp.linalg.cholesky(gram)
    solve = functools.partial(lax.linalg.triangular_solve, chol, left_side=False, lower=True, transpose_a=True)
    basis, cross = solve(power), solve(raw)
    q_next = cross / (jnp.sqrt(lax.psum(jnp.sum(cross * cross, axis=0), "cols")) + 1e-08)
    momentum_next = momentum - 0.5 * dot(basis, cross, NT)
    factor = momentum_prev.shape[0] * n_rows / jnp.sqrt(jnp.float32(q_prev.shape[1]))
    return momentum_next, q_next, (factor * dot(basis, q_next, NT)).astype(BF16)


def solution(mesh):
    n_rows, n_cols = mesh.shape["rows"], mesh.shape["cols"]

    def body(momentum_prev, gradient, q_prev):
        rows, cols = momentum_prev.shape
        block = rows // n_cols
        fits = (
            n_rows & (n_rows - 1) == 0
            and n_cols & (n_cols - 1) == 0
            and 4 <= n_cols <= CHUNK // 8
            and block % 128 == 0
            and cols % 128 == 0
            and q_prev.shape[1] % (4 * CHUNK) == 0
            and n_rows >= 2
        )
        return (fast if fits else plain)(n_rows, n_cols, momentum_prev, gradient, q_prev)

    in_specs = (P("rows", "cols"), P("rows", "cols"), P("cols", None))
    out_specs = (P("rows", "cols"), P("cols", None), P("rows", "cols"))
    return jax.shard_map(body, mesh=mesh, in_specs=in_specs, out_specs=out_specs, check_vma=False)
```

```python
import functools

import jax
import jax.numpy as jnp
from jax import lax
from jax.experimental import pallas as pl
from jax.experimental.pallas import tpu as pltpu
from jax.sharding import PartitionSpec as P

CHUNK = 128
SHRINK = 1
PANEL = 8
SCHEDULE = ['raw_a', 'slot', 'b', 'b', 'slot', 'b', 'gram', 'raw_b', 'gram', 'slot', 'gram', 'gram', 'gram', 'factor', 'slot', 'factor', 'slot', 'factor', 'slot', 'factor', 'basis', 'take']
F32, BF16 = jnp.float32, jnp.bfloat16
HIGHEST = lax.Precision.HIGHEST
NN = (((1,), (0,)), ((), ()))
NT = (((1,), (1,)), ((), ()))
MIB = 1024 * 1024
VMEM = pl.BlockSpec(memory_space=pltpu.VMEM)
SMEM = pl.BlockSpec(memory_space=pltpu.SMEM)
HBM = pl.BlockSpec(memory_space=pltpu.HBM)
DMA = pltpu.SemaphoreType.DMA


def params(mib):
    return pltpu.CompilerParams(vmem_limit_bytes=mib * MIB)


def shape(dims, dtype=F32):
    return jax.ShapeDtypeStruct(dims, dtype)


def cost(flops, nbytes):
    return pl.CostEstimate(flops=int(flops) // SHRINK, bytes_accessed=int(nbytes) // SHRINK, transcendentals=0)


def split(x):
    hi = x.astype(BF16)
    return hi, (x - hi.astype(F32)).astype(BF16)


def dot1(a, b, dims):
    return lax.dot_general(a, b, dims, preferred_element_type=F32)


def dot3(ah, al, bh, bl, dims=NN):
    return dot1(ah, bh, dims) + (dot1(al, bh, dims) + dot1(ah, bl, dims))


def dot_high(a, b, dims):
    return lax.dot_general(a, b, dims, precision=HIGHEST, preferred_element_type=F32)


def bit_orders(bits):
    rest = list(range(1, bits))
    half = (len(rest) + 1) // 2
    return rest, rest[half:] + rest[:half]


def position_masks(bits, parity):
    orders = bit_orders(bits)

    def walk(order):
        masks = [0]
        for bit in reversed(order):
            masks = masks + [m ^ (1 << bit) for m in masks]
        return masks

    return walk(orders[parity]) + [1 ^ m for m in walk(orders[1 - parity])]


def gathered_masks(bits, parity):
    masks = [0, 1]
    for bit in bit_orders(bits)[parity]:
        masks = masks + [m ^ (1 << bit) for m in masks]
    return masks


def pair_perms(bits):
    orders = bit_orders(bits)
    n = 1 << bits
    return [[(j, j ^ (1 << orders[j & 1][step])) for j in range(n)] for step in range(bits - 1)]


class Order:
    def __init__(self):
        self.token = None

    def __call__(self, f, *args):
        if self.token is not None:
            args, _ = lax.optimization_barrier((args, self.token))
        out = f(*args)
        self.token = jax.tree.leaves(out)[0]
        return out


def in_hbm(*xs):
    return [pltpu.with_memory_space_constraint(x, pltpu.HBM) for x in xs]


def in_vmem(*xs):
    return [pltpu.with_memory_space_constraint(x, pltpu.VMEM) for x in xs]


class Sent:
    def __init__(self, then, stages, x):
        self.then, self.stages = then, list(stages)
        self.send(x)

    def send(self, x):
        self.x = x
        if self.stages:
            self.received = lax.ppermute(x, *self.stages[0][1:])

    def step(self):
        if not self.stages:
            return
        combine = self.stages.pop(0)[0]
        self.send(self.then(combine, self.x, self.received))

    def finish(self):
        while self.stages:
            self.step()
        return self.x


def join(x, r):
    return jnp.concatenate([x, r], axis=0)


def xor_stages(combine, axis, n):
    bits = range(n.bit_length() - 1)
    return [(combine, axis, [(i, i ^ (1 << bit)) for i in range(n)]) for bit in bits]


def first_kernel(order_ref, mp_ref, g_ref, q_ref, hi_ref, lo_ref, keep_ref, send_ref, mb, gb, qb, qs, sm, sg, sq):
    half, width, block = keep_ref.shape

    def copies(t):
        rows = pl.ds(pl.multiple_of(order_ref[t] * block, block), block)
        return [
            pltpu.make_async_copy(mp_ref.at[rows, :], mb.at[t], sm.at[t]),
            pltpu.make_async_copy(g_ref.at[rows, :], gb.at[t], sg.at[t]),
        ]

    q_copy = pltpu.make_async_copy(q_ref, qb, sq)
    q_copy.start()
    for t in range(2 * half):
        for copy in copies(t):
            copy.start()
    q_copy.wait()
    qs[:, :width], qs[:, width:] = split(qb[:, :width])

    def part(out_ref, first, t):
        for copy in copies(first + t):
            copy.wait()
        h, l = split(0.95 * mb[first + t] + gb[first + t].astype(F32))
        rows = pl.ds(pl.multiple_of((first + t) * block, block), block)
        hi_ref[rows, :] = h
        lo_ref[rows, :] = l
        both = dot1(h, qs[...], NN)
        out_ref[t] = (both[:, :width] + (both[:, width:] + dot1(l, qs[:, :width], NN))).T

    for first, out_ref in ((0, keep_ref), (half, send_ref)):
        lax.fori_loop(0, half, lambda t, _: part(out_ref, first, t), None)


def first_call(order, mp, g, q, width):
    rows, cols = mp.shape
    blocks = order.shape[0]
    block, half = rows // blocks, blocks // 2
    return pl.pallas_call(
        first_kernel,
        in_specs=[SMEM, HBM, HBM, HBM],
        out_specs=[VMEM] * 4,
        out_shape=[pltpu.VMEM((rows, cols), BF16)] * 2 + [shape((half, width, block))] * 2,
        scratch_shapes=[
            pltpu.VMEM((blocks, block, cols), F32),
            pltpu.VMEM((blocks, block, cols), BF16),
            pltpu.VMEM(q.shape, F32),
            pltpu.VMEM((cols, 2 * width), BF16),
            DMA((blocks,)),
            DMA((blocks,)),
            DMA,
        ],
        compiler_params=params(26),
        cost_estimate=cost(6 * rows * cols * width, 6 * rows * cols),
        name="momentum_and_power",
    )(order, *in_hbm(mp, g, q))


def rest_kernel(hi_ref, lo_ref, q_ref, keep_ref, send_ref, qb, sem):
    half, width, block = keep_ref.shape
    copy = pltpu.make_async_copy(q_ref, qb, sem)
    copy.start()
    copy.wait()
    qh, ql = split(qb[:, qb.shape[1] - width :])
    for t in range(2 * half):
        rows = slice(t * block, (t + 1) * block)
        out_ref = keep_ref if t < half else send_ref
        out_ref[t % half] = dot3(hi_ref[rows, :], lo_ref[rows, :], qh, ql).T


def rest_call(hi, lo, q, width, blocks):
    rows, cols = hi.shape
    block, half = rows // blocks, blocks // 2
    return pl.pallas_call(
        rest_kernel,
        in_specs=[VMEM, VMEM, HBM],
        out_specs=[VMEM] * 2,
        out_shape=[shape((half, width, block))] * 2,
        scratch_shapes=[pltpu.VMEM(q.shape, F32), DMA],
        compiler_params=params(16),
        cost_estimate=cost(6 * rows * cols * width, 4 * rows * cols),
        name="power",
    )(*in_vmem(hi, lo), *in_hbm(q))


def raw_kernel(pa_ref, pb_ref, hi_ref, lo_ref, *refs):
    outs, acc = refs[:-1], refs[-1]
    half, width, block = pa_ref.shape
    for t in range(2 * half):
        ph, plo = split(pa_ref[t] if t < half else pb_ref[t - half])
        rows = slice(t * block, (t + 1) * block)
        both = dot1(jnp.concatenate([ph, plo], axis=0), hi_ref[rows, :], NN)
        term = both[:width] + (both[width:] + dot1(ph, lo_ref[rows, :], NN))
        acc[...] = term if t == 0 else acc[...] + term
    off = 0
    for out in outs:
        out[...] = acc[off : off + out.shape[0]]
        off += out.shape[0]


def raw_call(pa, pb, hi, lo, parts):
    rows, cols = hi.shape
    width = sum(parts)
    return pl.pallas_call(
        raw_kernel,
        in_specs=[VMEM] * 4,
        out_specs=[VMEM] * len(parts),
        out_shape=[shape((p, cols)) for p in parts],
        scratch_shapes=[pltpu.VMEM((width, cols), F32)],
        compiler_params=params(16),
        cost_estimate=cost(6 * rows * cols * width, 4 * rows * cols),
        name="raw",
    )(pa, pb, *in_vmem(hi, lo))


def split3(x):
    hi, lo = split(x)
    return hi, lo, (x - hi.astype(F32) - lo.astype(F32)).astype(BF16)


def gram_kernel(me_ref, *refs):
    pieces, out_ref = refs[:-1], refs[-1]
    half, width, _ = pieces[0].shape
    n = out_ref.shape[0] // 2
    mine = pl.ds(pl.multiple_of(me_ref[0] * n, n), n)
    sums = None
    for t in range(2 * half):
        refs = [p.at[t % half] for p in pieces[t // half :: 2]]
        x1, x2, x3 = split3(jnp.concatenate([r[...] for r in refs], axis=0))
        y = jnp.concatenate([r[mine, :] for r in refs], axis=0)
        y = jnp.concatenate(split3(y), axis=0)
        terms = [dot1(x1, y, NT), dot1(x2, y[: 4 * n], NT), dot1(x3, y[: 2 * n], NT)]
        sums = terms if sums is None else [s + u for s, u in zip(sums, terms)]
    z1, z2, z3 = sums
    n = 2 * n
    small = z1[:, 2 * n :] + (z2[:, n:] + z3)
    out_ref[...] = (z1[:, :n] + ((z1[:, n : 2 * n] + z2[:, :n]) + small)).T


def gram_call(me, pa, pb):
    refs = [*pa, *pb]
    half, width, block = refs[0].shape
    return pl.pallas_call(
        gram_kernel,
        in_specs=[SMEM] + [VMEM] * 4,
        out_specs=VMEM,
        out_shape=shape((width // half, 2 * width)),
        compiler_params=params(16),
        cost_estimate=cost(4e9, 32 * half * block * width),
        name="gram",
    )(me, *refs)


def eliminate(s_ref, w_ref):
    n = s_ref.shape[0]
    row = lax.broadcasted_iota(jnp.int32, (n, n), 0)
    col = lax.broadcasted_iota(jnp.int32, (n, n), 1)
    w_ref[...] = (row == col).astype(F32)
    full = (PANEL, n)
    sub = lax.broadcasted_iota(jnp.int32, full, 0)
    for base in range(0, n, PANEL):
        panel = s_ref[base : base + PANEL, :]
        wpanel = w_ref[base : base + PANEL, :]
        rows = [jnp.broadcast_to(panel[i : i + 1, :], full) for i in range(PANEL)]
        wrows = [jnp.broadcast_to(wpanel[i : i + 1, :], full) for i in range(PANEL)]
        v = {}
        for i in range(PANEL):
            for k in range(i, PANEL):
                v[i, k] = jnp.broadcast_to(rows[i][:, base + k : base + k + 1], full)
        mult, inv = {}, []
        for i in range(PANEL):
            r = 1.0 / v[i, i]
            inv.append(r)
            for a in range(i + 1, PANEL):
                m = v[i, a] * r
                mult[i, a] = m
                for k in range(a, PANEL):
                    v[a, k] = v[a, k] - m * v[i, k]
                rows[a] = rows[a] - m * rows[i]
                wrows[a] = wrows[a] - m * wrows[i]
        out = wrows[0] * lax.rsqrt(v[0, 0])
        for i in range(1, PANEL):
            out = jnp.where(sub == i, wrows[i] * lax.rsqrt(v[i, i]), out)
        w_ref[base : base + PANEL, :] = out
        for below in range(base + PANEL, n, PANEL):
            s = s_ref[below : below + PANEL, :]
            w = w_ref[below : below + PANEL, :]
            f = [jnp.broadcast_to(s[:, base + i : base + i + 1], full) for i in range(PANEL)]
            for i in range(PANEL):
                for a in range(i + 1, PANEL):
                    f[a] = f[a] - mult[i, a] * f[i]
            for i in range(PANEL):
                g = f[i] * inv[i]
                s = s - g * rows[i]
                w = w - g * wrows[i]
            s_ref[below : below + PANEL, :] = s
            w_ref[below : below + PANEL, :] = w


def chol_kernel(base, order_ref, own_ref, other_ref, *refs):
    prev = refs[0] if base else None
    out_ref, g_ref, s_ref, w_ref = refs[1 if base else 0 :]
    n = order_ref.shape[0]
    rows = own_ref.shape[0] // n
    here = slice(base, base + CHUNK)
    for i in range(CHUNK // rows):
        at = base // rows + i
        block = order_ref[at % n]
        local = pl.ds(pl.multiple_of((block % (n // 2) * 2 + at // n) * rows, rows), rows)
        own, other = own_ref[local, : base + CHUNK], other_ref[local, : base + CHUNK]
        g_ref[i * rows : (i + 1) * rows, :] = jnp.where(block < n // 2, own, other)
    s = g_ref[:, here]
    if base:
        before = prev[...]
        lrow = dot_high(g_ref[:, :base], before, NT)
        s = s - dot_high(lrow, lrow, NT)
    s_ref[...] = s
    eliminate(s_ref, w_ref)
    w = w_ref[...]
    out_ref[here, here] = w
    if base:
        out_ref[:base, :base] = before
        out_ref[:base, here] = jnp.zeros((base, CHUNK), F32)
        out_ref[here, :base] = -dot_high(w, dot_high(lrow, before, NN), NN)


def chol_call(order, own, other, prev):
    base = prev.shape[0] if prev is not None else 0
    size = base + CHUNK
    args = [own, other] + ([prev] if base else [])
    return pl.pallas_call(
        functools.partial(chol_kernel, base),
        in_specs=[SMEM] + [VMEM] * len(args),
        out_specs=VMEM,
        out_shape=shape((size, size)),
        scratch_shapes=[pltpu.VMEM((CHUNK, size), F32)] + [pltpu.VMEM((CHUNK, CHUNK), F32)] * 2,
        compiler_params=params(8),
        cost_estimate=cost(6e9, 8 * size * size),
        name="chol",
    )(order, *args)


def basis_kernel(inv_ref, *refs):
    pieces, (bh_ref, bl_ref) = refs[:-2], refs[-2:]
    half, _, block = pieces[0].shape
    ih, il = split(inv_ref[...])
    for t in range(2 * half):
        ph, plo = split(jnp.concatenate([p[t % half] for p in pieces[t // half :: 2]], axis=0))
        rows = slice(t * block, (t + 1) * block)
        bh_ref[rows, :], bl_ref[rows, :] = split(dot3(ih, il, ph, plo).T)


def basis_call(inv, pa, pb):
    half, width, block = pa[0].shape
    return pl.pallas_call(
        basis_kernel,
        in_specs=[VMEM] * 5,
        out_specs=[VMEM, VMEM],
        out_shape=[pltpu.VMEM((2 * half * block, 2 * width), BF16)] * 2,
        compiler_params=params(16),
        cost_estimate=cost(48 * width * width * block * half, 32 * width * block * half),
        name="basis",
    )(inv, *pa, *pb)


def cross_kernel(skip, inv_ref, *refs):
    raws, (out_ref, ch_ref, cl_ref, sq_ref) = refs[:-4], refs[-4:]
    size = skip + out_ref.shape[0]
    ih, il = split(inv_ref[skip:size, :size])
    rh, rl = split(jnp.concatenate([r[...] for r in raws], axis=0))
    cross = dot3(ih, il, rh, rl)
    out_ref[...] = cross
    ch_ref[...], cl_ref[...] = split(cross)
    sq_ref[...] = jnp.sum(cross * cross, axis=1, keepdims=True).T


def cross_call(inv, raws, skip):
    cols = raws[0].shape[1]
    rows = sum(r.shape[0] for r in raws) - skip
    return pl.pallas_call(
        functools.partial(cross_kernel, skip),
        in_specs=[VMEM] * (1 + len(raws)),
        out_specs=[VMEM] * 4,
        out_shape=[pltpu.VMEM((rows, cols), F32), pltpu.VMEM((rows, cols), BF16), pltpu.VMEM((rows, cols), BF16), shape((1, rows))],
        compiler_params=params(16),
        cost_estimate=cost(6 * rows * (rows + skip) * cols, 8 * rows * cols),
        name="cross",
    )(inv, *raws)


def store_rows(order_ref, place, buf, t, out_ref, sem):
    block = buf.shape[1]
    rows = pl.ds(pl.multiple_of(order_ref[place] * block, block), block)
    copy = pltpu.make_async_copy(buf.at[t], out_ref.at[rows, :], sem.at[t])
    copy.start()
    return copy


def momentum_kernel(first, order_ref, bh_ref, bl_ref, hi_ref, lo_ref, ch_ref, cl_ref, *refs):
    out_ref, buf, sem = refs[-3:]
    blocks, block, _ = buf.shape
    copies = []
    for t in range(blocks):
        rows = slice((first + t) * block, (first + t + 1) * block)
        prod = dot3(bh_ref[rows, :], bl_ref[rows, :], ch_ref[...], cl_ref[...])
        buf[t] = (hi_ref[rows, :].astype(F32) + lo_ref[rows, :].astype(F32)) - 0.5 * prod
        copies.append(store_rows(order_ref, first + t, buf, t, out_ref, sem))
    for copy in copies:
        copy.wait()


def momentum_call(order, bh, bl, hi, lo, ch, cl, first, so_far):
    rows, cols = hi.shape
    rank, blocks = bh.shape[1], order.shape[0]
    more = [] if so_far is None else [so_far]
    args = in_vmem(bh, bl, hi, lo, ch, cl)
    return pl.pallas_call(
        functools.partial(momentum_kernel, first),
        in_specs=[SMEM] + [VMEM] * len(args) + [HBM] * len(more),
        out_specs=HBM,
        out_shape=shape((rows, cols)),
        scratch_shapes=[pltpu.VMEM((blocks // 2, rows // blocks, cols), F32), DMA((blocks // 2,))],
        input_output_aliases={1 + len(args): 0} if more else {},
        compiler_params=params(12),
        cost_estimate=cost(3 * rows * cols * rank, 4 * rows * cols),
        name="momentum_next",
    )(order, *args, *more)


def update_kernel(factor, order_ref, bh_ref, bl_ref, c_ref, ch_ref, cl_ref, sq_ref, out_ref, qn_ref, buf, qbuf, sem, qsem):
    blocks, block, cols = buf.shape
    scale = 1.0 / (jnp.sqrt(sq_ref[...]) + 1e-08)
    copies = []
    step = cols // blocks
    for t in range(blocks):
        rows = slice(t * block, (t + 1) * block)
        bh, bl = split((bh_ref[rows, :].astype(F32) + bl_ref[rows, :].astype(F32)) * scale)
        prod = dot3(bh, bl, ch_ref[...], cl_ref[...])
        buf[t] = (factor * prod).astype(BF16)
        copies.append(store_rows(order_ref, t, buf, t, out_ref, sem))
        qbuf[t] = c_ref[:, t * step : (t + 1) * step].T * scale
        copy = pltpu.make_async_copy(qbuf.at[t], qn_ref.at[pl.ds(t * step, step), :], qsem.at[t])
        copy.start()
        copies.append(copy)
    for copy in copies:
        copy.wait()


def update_call(order, bh, bl, cross, ch, cl, sq, factor):
    rows, rank = bh.shape
    cols, blocks = cross.shape[1], order.shape[0]
    return pl.pallas_call(
        functools.partial(update_kernel, factor),
        in_specs=[SMEM] + [VMEM] * 6,
        out_specs=[HBM, HBM],
        out_shape=[shape((rows, cols), BF16), shape((cols, rank))],
        scratch_shapes=[
            pltpu.VMEM((blocks, rows // blocks, cols), BF16),
            pltpu.VMEM((blocks, cols // blocks, rank), F32),
            DMA((blocks,)),
            DMA((blocks,)),
        ],
        compiler_params=params(16),
        cost_estimate=cost(6 * rows * cols * rank, 8 * rows * cols),
        name="update",
    )(order, *in_vmem(bh, bl, cross, ch, cl), sq)


def fast(n_rows, n_cols, momentum_prev, gradient, q_prev):
    rank = q_prev.shape[1]
    width = rank // 2
    bits = n_cols.bit_length() - 1
    me = lax.axis_index("cols").astype(jnp.int32)
    masks = jnp.where(
        me % 2 == 0,
        jnp.array(position_masks(bits, 0), jnp.int32),
        jnp.array(position_masks(bits, 1), jnp.int32),
    )
    order = me ^ masks
    places = [[gathered_masks(bits, p).index(m) for m in range(n_cols)] for p in range(2)]
    places = jnp.where(me % 2 == 0, jnp.array(places[0], jnp.int32), jnp.array(places[1], jnp.int32))
    gram_order = places[me ^ jnp.arange(n_cols, dtype=jnp.int32)]
    core = [(j, j ^ 1) for j in range(n_cols)]
    perms = pair_perms(bits)
    then = Order()

    def halve(k, r):
        n = k.shape[0] // 2
        return k[n:] + r[n:], k[:n] + r[:n]

    hi, lo, keep, send = then(lambda *x: first_call(*x, width), order, momentum_prev, gradient, q_prev)
    s, a = then(halve, keep, lax.ppermute(send, "cols", core))
    ra = lax.ppermute(s, "cols", perms[0])
    keep, send = then(lambda *x: rest_call(*x, rank - width, n_cols), hi, lo, q_prev)
    rb = lax.ppermute(send, "cols", core)
    s, a = then(halve, a, ra)
    a = then(jnp.add, a, lax.ppermute(s, "cols", perms[1]))
    ra = lax.ppermute(a, "cols", perms[1])

    def both_steps(a, ra, b, rb):
        s, b = halve(b, rb)
        a = join(a, ra)
        return join(a, s), a, b

    s, a, b = then(both_steps, a, ra, keep, rb)
    s = lax.ppermute(s, "cols", perms[0])
    n = a.shape[0]
    a = then(lambda a, s: join(a, s[:n]), a, s)
    pa = (a, lax.ppermute(a, "cols", core))
    s, b = then(halve, b, s[n:])
    state = {"inv": None, "b": b, "rb": lax.ppermute(s, "cols", perms[1])}
    later = [(jnp.add, perms[1]), (join, perms[0]), (join, core)]

    def step_b():
        f, perm = later.pop(0)
        state["b"] = then(f, state["b"], state["rb"])
        state["rb"] = lax.ppermute(state["b"], "cols", perm)
        state["pb"] = (state["b"], state["rb"])

    gram_stages = xor_stages(jnp.add, "rows", n_rows) + [(join, "cols", perm) for perm in [core] + perms]
    norm_stages = xor_stages(jnp.add, "cols", n_cols)
    sizes = [CHUNK] * (width // CHUNK)
    z = lax.axis_index("rows")
    ends = (z == 0) | (z == n_rows - 1)
    outer = [(i, i ^ 1) for i in range(n_rows)]
    inner = [(1, 2), (2, 1)]

    def raw(half):
        out = then(lambda *x: raw_call(*x, sizes), *state["p" + half], hi, lo)
        for i, piece in enumerate(out):
            state[f"{half}{i}"] = piece

    def gram():
        if "gram" in state:
            state["gram"].step()
        else:
            x = then(lambda m, *p: gram_call(m, p[:2], p[2:]), me.reshape(1), *pa, *state["pb"])
            state["gram"] = Sent(then, gram_stages, x)

    def factor():
        g, prev = state["gram"], [] if state["inv"] is None else [state["inv"]]
        state["inv"] = then(lambda o, *g: chol_call(o, *g[:2], *(g[2:] or [None])), gram_order, g.x, g.received, *prev)

    def basis():
        state["basis"] = then(lambda i, *p: basis_call(i, p[:2], p[2:]), state["inv"], *pa, *state["pb"])

    def send_outer(new, old):
        both = [state[k] for k in (new, old) if k]
        x = then(lambda *p: jnp.where(ends, p[0], p[-1]) if len(p) > 1 else p[0], *both)
        state["outer"] = (new, old, lax.ppermute(x, "rows", outer))

    def take_outer():
        new, old, r = state["outer"]
        if new:
            state[new] = then(lambda x, r: jnp.where(ends, x, x + r), state[new], r)
        if old:
            state[old] = then(lambda x, r: jnp.where(ends, r, x), state[old], r)

    def send_inner(k):
        state["inner"] = (k, lax.ppermute(state[k], "rows", inner))

    def take_inner():
        k, r = state["inner"]
        state[k] = then(jnp.add, state[k], r)

    state["pa"] = pa
    names = [f"{half}{i}" for half in "ab" for i in range(len(sizes))]
    parts = names + [None, None]

    count = iter(range(len(parts)))

    def take():
        if "outer" in state:
            take_outer()
            del state["outer"]
        if "inner" in state:
            take_inner()
            del state["inner"]

    def slot():
        take()
        k = next(count)
        send_outer(parts[k], names[k - 2] if k > 1 else None)
        if 0 < k <= len(names):
            send_inner(names[k - 1])

    steps = {"raw_a": lambda: raw("a"), "raw_b": lambda: raw("b"), "b": step_b, "gram": gram}
    steps |= {"factor": factor, "basis": basis, "slot": slot, "take": take}
    for name in SCHEDULE:
        steps[name]()
    inv, (bh, bl) = state["inv"], state["basis"]
    raws = [state[name] for name in names]
    cross, ch, cl, sq = then(lambda i, *r: cross_call(i, r, 0), inv, *raws)
    norm = Sent(then, norm_stages, sq)
    norm.step()
    part = then(lambda *x: momentum_call(*x, 0, None), order, bh, bl, hi, lo, ch, cl)
    norm.step()
    momentum_next = then(lambda p, *x: momentum_call(*x, n_cols // 2, p), part, order, bh, bl, hi, lo, ch, cl)
    scale = momentum_prev.shape[0] * n_rows / rank**0.5
    update, q_next = then(lambda *x: update_call(*x, scale), order, bh, bl, cross, ch, cl, norm.finish())
    return momentum_next, q_next, update


def plain(n_rows, n_cols, momentum_prev, gradient, q_prev):
    high = lax.Precision.HIGHEST
    dot = functools.partial(lax.dot_general, precision=high, preferred_element_type=F32)
    momentum = 0.95 * momentum_prev + gradient.astype(F32)
    power = lax.psum_scatter(dot(momentum, q_prev, NN), "cols", scatter_dimension=0, tiled=True)
    power = lax.all_gather(power, "cols", axis=0, tiled=True)
    tn = (((0,), (0,)), ((), ()))
    raw, gram = lax.psum((dot(momentum, power, tn), dot(power, power, tn)), "rows")
    chol = jnp.linalg.cholesky(gram)
    solve = functools.partial(lax.linalg.triangular_solve, chol, left_side=False, lower=True, transpose_a=True)
    basis, cross = solve(power), solve(raw)
    q_next = cross / (jnp.sqrt(lax.psum(jnp.sum(cross * cross, axis=0), "cols")) + 1e-08)
    momentum_next = momentum - 0.5 * dot(basis, cross, NT)
    factor = momentum_prev.shape[0] * n_rows / jnp.sqrt(jnp.float32(q_prev.shape[1]))
    return momentum_next, q_next, (factor * dot(basis, q_next, NT)).astype(BF16)


def solution(mesh):
    n_rows, n_cols = mesh.shape["rows"], mesh.shape["cols"]

    def body(momentum_prev, gradient, q_prev):
        rows, cols = momentum_prev.shape
        block = rows // n_cols
        fits = (
            n_rows == 4
            and n_cols == 8
            and block % 128 == 0
            and cols % 128 == 0
            and q_prev.shape[1] % (4 * CHUNK) == 0
        )
        return (fast if fits else plain)(n_rows, n_cols, momentum_prev, gradient, q_prev)

    in_specs = (P("rows", "cols"), P("rows", "cols"), P("cols", None))
    out_specs = (P("rows", "cols"), P("cols", None), P("rows", "cols"))
    return jax.shard_map(body, mesh=mesh, in_specs=in_specs, out_specs=out_specs, check_vma=False)
```

```python
import functools

import jax
import jax.numpy as jnp
from jax import lax
from jax.experimental import pallas as pl
from jax.experimental.pallas import tpu as pltpu
from jax.sharding import PartitionSpec as P

CHUNK = 128
SHRINK = 1
PANEL = 8
SCHEDULE = [
    *["raw_a", "slot", "b", "b", "slot", "b", "gram", "raw_b", "gram", "slot", "gram", "gram", "factor"],
    *["slot", "factor", "slot", "factor", "slot", "factor", "basis", "take"],
]
F32, BF16 = jnp.float32, jnp.bfloat16
HIGHEST = lax.Precision.HIGHEST
NN = (((1,), (0,)), ((), ()))
NT = (((1,), (1,)), ((), ()))
MIB = 1024 * 1024
VMEM = pl.BlockSpec(memory_space=pltpu.VMEM)
SMEM = pl.BlockSpec(memory_space=pltpu.SMEM)
HBM = pl.BlockSpec(memory_space=pltpu.HBM)
DMA = pltpu.SemaphoreType.DMA


def params(mib):
    return pltpu.CompilerParams(vmem_limit_bytes=mib * MIB)


def shape(dims, dtype=F32):
    return jax.ShapeDtypeStruct(dims, dtype)


def cost(flops, nbytes):
    return pl.CostEstimate(flops=int(flops) // SHRINK, bytes_accessed=int(nbytes) // SHRINK, transcendentals=0)


def split(x):
    hi = x.astype(BF16)
    return hi, (x - hi.astype(F32)).astype(BF16)


def dot1(a, b, dims):
    return lax.dot_general(a, b, dims, preferred_element_type=F32)


def dot3(ah, al, bh, bl, dims=NN):
    return dot1(ah, bh, dims) + (dot1(al, bh, dims) + dot1(ah, bl, dims))


def dot_high(a, b, dims):
    return lax.dot_general(a, b, dims, precision=HIGHEST, preferred_element_type=F32)


def bit_orders(bits):
    rest = list(range(1, bits))
    half = (len(rest) + 1) // 2
    return rest, rest[half:] + rest[:half]


def position_masks(bits, parity):
    orders = bit_orders(bits)

    def walk(order):
        masks = [0]
        for bit in reversed(order):
            masks = masks + [m ^ (1 << bit) for m in masks]
        return masks

    return walk(orders[parity]) + [1 ^ m for m in walk(orders[1 - parity])]


def pair_perms(bits):
    orders = bit_orders(bits)
    n = 1 << bits
    return [[(j, j ^ (1 << orders[j & 1][step])) for j in range(n)] for step in range(bits - 1)]


class Order:
    def __init__(self):
        self.token = None

    def __call__(self, f, *args):
        if self.token is not None:
            args, _ = lax.optimization_barrier((args, self.token))
        out = f(*args)
        self.token = jax.tree.leaves(out)[0]
        return out


def in_hbm(*xs):
    return [pltpu.with_memory_space_constraint(x, pltpu.HBM) for x in xs]


def in_vmem(*xs):
    return [pltpu.with_memory_space_constraint(x, pltpu.VMEM) for x in xs]


class Sent:
    def __init__(self, then, stages, x):
        self.then, self.stages = then, list(stages)
        self.send(x)

    def send(self, x):
        self.x = x
        if self.stages:
            self.received = lax.ppermute(x, *self.stages[0][1:])

    def step(self):
        if not self.stages:
            return
        combine = self.stages.pop(0)[0]
        self.send(self.then(combine, self.x, self.received))

    def finish(self):
        while self.stages:
            self.step()
        return self.x


def join(x, r):
    return jnp.concatenate([x, r], axis=0)


def xor_stages(combine, axis, n):
    bits = range(n.bit_length() - 1)
    return [(combine, axis, [(i, i ^ (1 << bit)) for i in range(n)]) for bit in bits]


def first_kernel(order_ref, mp_ref, g_ref, q_ref, hi_ref, lo_ref, keep_ref, send_ref, mb, gb, qb, qs, sm, sg, sq):
    half, width, block = keep_ref.shape

    def copies(t):
        rows = pl.ds(pl.multiple_of(order_ref[t] * block, block), block)
        return [
            pltpu.make_async_copy(mp_ref.at[rows, :], mb.at[t], sm.at[t]),
            pltpu.make_async_copy(g_ref.at[rows, :], gb.at[t], sg.at[t]),
        ]

    q_copy = pltpu.make_async_copy(q_ref, qb, sq)
    q_copy.start()
    for t in range(2 * half):
        for copy in copies(t):
            copy.start()
    q_copy.wait()
    qs[:, :width], qs[:, width:] = split(qb[:, :width])

    def part(out_ref, first, t):
        for copy in copies(first + t):
            copy.wait()
        h, l = split(0.95 * mb[first + t] + gb[first + t].astype(F32))
        rows = pl.ds(pl.multiple_of((first + t) * block, block), block)
        hi_ref[rows, :] = h
        lo_ref[rows, :] = l
        both = dot1(h, qs[...], NN)
        out_ref[t] = (both[:, :width] + (both[:, width:] + dot1(l, qs[:, :width], NN))).T

    for first, out_ref in ((0, keep_ref), (half, send_ref)):
        lax.fori_loop(0, half, lambda t, _: part(out_ref, first, t), None)


def first_call(order, mp, g, q, width):
    rows, cols = mp.shape
    blocks = order.shape[0]
    block, half = rows // blocks, blocks // 2
    return pl.pallas_call(
        first_kernel,
        in_specs=[SMEM, HBM, HBM, HBM],
        out_specs=[VMEM] * 4,
        out_shape=[pltpu.VMEM((rows, cols), BF16)] * 2 + [shape((half, width, block))] * 2,
        scratch_shapes=[
            pltpu.VMEM((blocks, block, cols), F32),
            pltpu.VMEM((blocks, block, cols), BF16),
            pltpu.VMEM(q.shape, F32),
            pltpu.VMEM((cols, 2 * width), BF16),
            DMA((blocks,)),
            DMA((blocks,)),
            DMA,
        ],
        compiler_params=params(26),
        cost_estimate=cost(6 * rows * cols * width, 6 * rows * cols),
        name="momentum_and_power",
    )(order, *in_hbm(mp, g, q))


def rest_kernel(hi_ref, lo_ref, q_ref, keep_ref, send_ref, qb, sem):
    half, width, block = keep_ref.shape
    copy = pltpu.make_async_copy(q_ref, qb, sem)
    copy.start()
    copy.wait()
    qh, ql = split(qb[:, qb.shape[1] - width :])
    for t in range(2 * half):
        rows = slice(t * block, (t + 1) * block)
        out_ref = keep_ref if t < half else send_ref
        out_ref[t % half] = dot3(hi_ref[rows, :], lo_ref[rows, :], qh, ql).T


def rest_call(hi, lo, q, width, blocks):
    rows, cols = hi.shape
    block, half = rows // blocks, blocks // 2
    return pl.pallas_call(
        rest_kernel,
        in_specs=[VMEM, VMEM, HBM],
        out_specs=[VMEM] * 2,
        out_shape=[shape((half, width, block))] * 2,
        scratch_shapes=[pltpu.VMEM(q.shape, F32), DMA],
        compiler_params=params(16),
        cost_estimate=cost(6 * rows * cols * width, 4 * rows * cols),
        name="power",
    )(*in_vmem(hi, lo), *in_hbm(q))


def raw_kernel(pa_ref, pb_ref, hi_ref, lo_ref, *refs):
    outs, acc = refs[:-1], refs[-1]
    half, width, block = pa_ref.shape
    for t in range(2 * half):
        ph, plo = split(pa_ref[t] if t < half else pb_ref[t - half])
        rows = slice(t * block, (t + 1) * block)
        both = dot1(jnp.concatenate([ph, plo], axis=0), hi_ref[rows, :], NN)
        term = both[:width] + (both[width:] + dot1(ph, lo_ref[rows, :], NN))
        acc[...] = term if t == 0 else acc[...] + term
    off = 0
    for out in outs:
        out[...] = acc[off : off + out.shape[0]]
        off += out.shape[0]


def raw_call(pa, pb, hi, lo, parts):
    rows, cols = hi.shape
    width = sum(parts)
    return pl.pallas_call(
        raw_kernel,
        in_specs=[VMEM] * 4,
        out_specs=[VMEM] * len(parts),
        out_shape=[shape((p, cols)) for p in parts],
        scratch_shapes=[pltpu.VMEM((width, cols), F32)],
        compiler_params=params(16),
        cost_estimate=cost(6 * rows * cols * width, 4 * rows * cols),
        name="raw",
    )(pa, pb, *in_vmem(hi, lo))


def split3(x):
    hi, lo = split(x)
    return hi, lo, (x - hi.astype(F32) - lo.astype(F32)).astype(BF16)


def gram_kernel(me_ref, *refs):
    pieces, out_ref = refs[:-1], refs[-1]
    half, width, _ = pieces[0].shape
    n = out_ref.shape[0]
    mine = pl.ds(pl.multiple_of(me_ref[0] * n, n), n)
    sums = None
    for t in range(2 * half):
        refs = [p.at[t % half] for p in pieces[t // half :: 2]]
        x1, x2, x3 = split3(jnp.concatenate([r[...] for r in refs], axis=0))
        y = jnp.concatenate([r[mine, :] for r in refs], axis=0)
        y = jnp.concatenate(split3(y), axis=0)
        terms = [dot1(x1, y, NT), dot1(x2, y[: 4 * n], NT), dot1(x3, y[: 2 * n], NT)]
        sums = terms if sums is None else [s + u for s, u in zip(sums, terms)]
    z1, z2, z3 = sums
    n = 2 * n
    small = z1[:, 2 * n :] + (z2[:, n:] + z3)
    rows = (z1[:, :n] + ((z1[:, n : 2 * n] + z2[:, :n]) + small)).T
    out_ref[:, : 2 * width] = rows[n // 2 :]
    out_ref[:, 2 * width :] = rows[: n // 2, :width]


def gram_call(me, pa, pb):
    refs = [*pa, *pb]
    half, width, block = refs[0].shape
    return pl.pallas_call(
        gram_kernel,
        in_specs=[SMEM] + [VMEM] * 4,
        out_specs=VMEM,
        out_shape=shape((width // (2 * half), 3 * width)),
        compiler_params=params(16),
        cost_estimate=cost(4e9, 32 * half * block * width),
        name="gram",
    )(me, *refs)


def eliminate(s_ref, w_ref):
    n = s_ref.shape[0]
    row = lax.broadcasted_iota(jnp.int32, (n, n), 0)
    col = lax.broadcasted_iota(jnp.int32, (n, n), 1)
    w_ref[...] = (row == col).astype(F32)
    full = (PANEL, n)
    sub = lax.broadcasted_iota(jnp.int32, full, 0)
    for base in range(0, n, PANEL):
        panel = s_ref[base : base + PANEL, :]
        wpanel = w_ref[base : base + PANEL, :]
        rows = [jnp.broadcast_to(panel[i : i + 1, :], full) for i in range(PANEL)]
        wrows = [jnp.broadcast_to(wpanel[i : i + 1, :], full) for i in range(PANEL)]
        v = {}
        for i in range(PANEL):
            for k in range(i, PANEL):
                v[i, k] = jnp.broadcast_to(rows[i][:, base + k : base + k + 1], full)
        mult, inv = {}, []
        for i in range(PANEL):
            r = 1.0 / v[i, i]
            inv.append(r)
            for a in range(i + 1, PANEL):
                m = v[i, a] * r
                mult[i, a] = m
                for k in range(a, PANEL):
                    v[a, k] = v[a, k] - m * v[i, k]
                rows[a] = rows[a] - m * rows[i]
                wrows[a] = wrows[a] - m * wrows[i]
        out = wrows[0] * lax.rsqrt(v[0, 0])
        for i in range(1, PANEL):
            out = jnp.where(sub == i, wrows[i] * lax.rsqrt(v[i, i]), out)
        w_ref[base : base + PANEL, :] = out
        for below in range(base + PANEL, n, PANEL):
            s = s_ref[below : below + PANEL, :]
            w = w_ref[below : below + PANEL, :]
            f = [jnp.broadcast_to(s[:, base + i : base + i + 1], full) for i in range(PANEL)]
            for i in range(PANEL):
                for a in range(i + 1, PANEL):
                    f[a] = f[a] - mult[i, a] * f[i]
            for i in range(PANEL):
                g = f[i] * inv[i]
                s = s - g * rows[i]
                w = w - g * wrows[i]
            s_ref[below : below + PANEL, :] = s
            w_ref[below : below + PANEL, :] = w


def chol_kernel(base, n_pairs, order_ref, *refs):
    pairs, refs = refs[:n_pairs], refs[n_pairs:]
    prev = refs[0] if base else None
    out_ref, g_ref, s_ref, w_ref = refs[1 if base else 0 :]
    rows, width = pairs[0].shape[0] // 2, pairs[0].shape[1] // 3
    here, end = slice(base, base + CHUNK), base + CHUNK
    lanes = slice(0, end) if base >= width else slice(2 * width, 2 * width + end)
    for i in range(CHUNK // rows):
        mask = order_ref[base // rows % (2 * n_pairs) + i]
        local = pl.ds(pl.multiple_of(mask % 2 * rows, rows), rows)
        piece = pairs[0][local, lanes]
        for p in range(1, n_pairs):
            piece = jnp.where(mask // 2 == p, pairs[p][local, lanes], piece)
        g_ref[i * rows : (i + 1) * rows, :] = piece
    s = g_ref[:, here]
    if base:
        before = prev[...]
        lrow = dot_high(g_ref[:, :base], before, NT)
        s = s - dot_high(lrow, lrow, NT)
    s_ref[...] = s
    eliminate(s_ref, w_ref)
    w = w_ref[...]
    out_ref[here, here] = w
    if base:
        out_ref[:base, :base] = before
        out_ref[:base, here] = jnp.zeros((base, CHUNK), F32)
        out_ref[here, :base] = -dot_high(w, dot_high(lrow, before, NN), NN)


def chol_call(order, pairs, prev):
    base = prev.shape[0] if prev is not None else 0
    size = base + CHUNK
    args = list(pairs) + ([prev] if base else [])
    return pl.pallas_call(
        functools.partial(chol_kernel, base, len(pairs)),
        in_specs=[SMEM] + [VMEM] * len(args),
        out_specs=VMEM,
        out_shape=shape((size, size)),
        scratch_shapes=[pltpu.VMEM((CHUNK, size), F32)] + [pltpu.VMEM((CHUNK, CHUNK), F32)] * 2,
        compiler_params=params(8),
        cost_estimate=cost(6e9, 8 * size * size),
        name="chol",
    )(order, *args)


def basis_kernel(inv_ref, *refs):
    pieces, (bh_ref, bl_ref) = refs[:-2], refs[-2:]
    half, _, block = pieces[0].shape
    ih, il = split(inv_ref[...])
    for t in range(2 * half):
        ph, plo = split(jnp.concatenate([p[t % half] for p in pieces[t // half :: 2]], axis=0))
        rows = slice(t * block, (t + 1) * block)
        bh_ref[rows, :], bl_ref[rows, :] = split(dot3(ih, il, ph, plo).T)


def basis_call(inv, pa, pb):
    half, width, block = pa[0].shape
    return pl.pallas_call(
        basis_kernel,
        in_specs=[VMEM] * 5,
        out_specs=[VMEM, VMEM],
        out_shape=[pltpu.VMEM((2 * half * block, 2 * width), BF16)] * 2,
        compiler_params=params(16),
        cost_estimate=cost(48 * width * width * block * half, 32 * width * block * half),
        name="basis",
    )(inv, *pa, *pb)


def cross_kernel(skip, inv_ref, *refs):
    raws, (out_ref, ch_ref, cl_ref, sq_ref) = refs[:-4], refs[-4:]
    size = skip + out_ref.shape[0]
    ih, il = split(inv_ref[skip:size, :size])
    rh, rl = split(jnp.concatenate([r[...] for r in raws], axis=0))
    cross = dot3(ih, il, rh, rl)
    out_ref[...] = cross
    ch_ref[...], cl_ref[...] = split(cross)
    sq_ref[...] = jnp.sum(cross * cross, axis=1, keepdims=True).T


def cross_call(inv, raws, skip):
    cols = raws[0].shape[1]
    rows = sum(r.shape[0] for r in raws) - skip
    return pl.pallas_call(
        functools.partial(cross_kernel, skip),
        in_specs=[VMEM] * (1 + len(raws)),
        out_specs=[VMEM] * 4,
        out_shape=[pltpu.VMEM((rows, cols), F32), pltpu.VMEM((rows, cols), BF16), pltpu.VMEM((rows, cols), BF16), shape((1, rows))],
        compiler_params=params(16),
        cost_estimate=cost(6 * rows * (rows + skip) * cols, 8 * rows * cols),
        name="cross",
    )(inv, *raws)


def store_rows(order_ref, place, buf, t, out_ref, sem):
    block = buf.shape[1]
    rows = pl.ds(pl.multiple_of(order_ref[place] * block, block), block)
    copy = pltpu.make_async_copy(buf.at[t], out_ref.at[rows, :], sem.at[t])
    copy.start()
    return copy


def momentum_kernel(first, order_ref, bh_ref, bl_ref, hi_ref, lo_ref, ch_ref, cl_ref, *refs):
    out_ref, buf, sem = refs[-3:]
    blocks, block, _ = buf.shape
    copies = []
    for t in range(blocks):
        rows = slice((first + t) * block, (first + t + 1) * block)
        prod = dot3(bh_ref[rows, :], bl_ref[rows, :], ch_ref[...], cl_ref[...])
        buf[t] = (hi_ref[rows, :].astype(F32) + lo_ref[rows, :].astype(F32)) - 0.5 * prod
        copies.append(store_rows(order_ref, first + t, buf, t, out_ref, sem))
    for copy in copies:
        copy.wait()


def momentum_call(order, bh, bl, hi, lo, ch, cl, first, so_far):
    rows, cols = hi.shape
    rank, blocks = bh.shape[1], order.shape[0]
    more = [] if so_far is None else [so_far]
    args = in_vmem(bh, bl, hi, lo, ch, cl)
    return pl.pallas_call(
        functools.partial(momentum_kernel, first),
        in_specs=[SMEM] + [VMEM] * len(args) + [HBM] * len(more),
        out_specs=HBM,
        out_shape=shape((rows, cols)),
        scratch_shapes=[pltpu.VMEM((blocks // 2, rows // blocks, cols), F32), DMA((blocks // 2,))],
        input_output_aliases={1 + len(args): 0} if more else {},
        compiler_params=params(12),
        cost_estimate=cost(3 * rows * cols * rank, 4 * rows * cols),
        name="momentum_next",
    )(order, *args, *more)


def update_kernel(factor, order_ref, bh_ref, bl_ref, c_ref, ch_ref, cl_ref, sq_ref, out_ref, qn_ref, buf, qbuf, sem, qsem):
    blocks, block, cols = buf.shape
    scale = 1.0 / (jnp.sqrt(sq_ref[...]) + 1e-08)
    copies = []
    step = cols // blocks
    for t in range(blocks):
        rows = slice(t * block, (t + 1) * block)
        bh, bl = split((bh_ref[rows, :].astype(F32) + bl_ref[rows, :].astype(F32)) * scale)
        prod = dot3(bh, bl, ch_ref[...], cl_ref[...])
        buf[t] = (factor * prod).astype(BF16)
        copies.append(store_rows(order_ref, t, buf, t, out_ref, sem))
        qbuf[t] = c_ref[:, t * step : (t + 1) * step].T * scale
        copy = pltpu.make_async_copy(qbuf.at[t], qn_ref.at[pl.ds(t * step, step), :], qsem.at[t])
        copy.start()
        copies.append(copy)
    for copy in copies:
        copy.wait()


def update_call(order, bh, bl, cross, ch, cl, sq, factor):
    rows, rank = bh.shape
    cols, blocks = cross.shape[1], order.shape[0]
    return pl.pallas_call(
        functools.partial(update_kernel, factor),
        in_specs=[SMEM] + [VMEM] * 6,
        out_specs=[HBM, HBM],
        out_shape=[shape((rows, cols), BF16), shape((cols, rank))],
        scratch_shapes=[
            pltpu.VMEM((blocks, rows // blocks, cols), BF16),
            pltpu.VMEM((blocks, cols // blocks, rank), F32),
            DMA((blocks,)),
            DMA((blocks,)),
        ],
        compiler_params=params(16),
        cost_estimate=cost(6 * rows * cols * rank, 8 * rows * cols),
        name="update",
    )(order, *in_vmem(bh, bl, cross, ch, cl), sq)


def fast(n_rows, n_cols, momentum_prev, gradient, q_prev):
    rank = q_prev.shape[1]
    width = rank // 2
    bits = n_cols.bit_length() - 1
    me = lax.axis_index("cols").astype(jnp.int32)
    masks = jnp.where(
        me % 2 == 0,
        jnp.array(position_masks(bits, 0), jnp.int32),
        jnp.array(position_masks(bits, 1), jnp.int32),
    )
    order = me ^ masks
    xor_order = me ^ jnp.arange(n_cols, dtype=jnp.int32)
    core = [(j, j ^ 1) for j in range(n_cols)]
    perms = pair_perms(bits)
    then = Order()

    def halve(k, r):
        n = k.shape[0] // 2
        return k[n:] + r[n:], k[:n] + r[:n]

    hi, lo, keep, send = then(lambda *x: first_call(*x, width), order, momentum_prev, gradient, q_prev)
    s, a = then(halve, keep, lax.ppermute(send, "cols", core))
    ra = lax.ppermute(s, "cols", perms[0])
    keep, send = then(lambda *x: rest_call(*x, rank - width, n_cols), hi, lo, q_prev)
    rb = lax.ppermute(send, "cols", core)
    s, a = then(halve, a, ra)
    a = then(jnp.add, a, lax.ppermute(s, "cols", perms[1]))
    ra = lax.ppermute(a, "cols", perms[1])

    def both_steps(a, ra, b, rb):
        s, b = halve(b, rb)
        a = join(a, ra)
        return join(a, s), a, b

    s, a, b = then(both_steps, a, ra, keep, rb)
    s = lax.ppermute(s, "cols", perms[0])
    n = a.shape[0]
    a = then(lambda a, s: join(a, s[:n]), a, s)
    pa = (a, lax.ppermute(a, "cols", core))
    s, b = then(halve, b, s[n:])
    state = {"inv": None, "b": b, "rb": lax.ppermute(s, "cols", perms[1])}
    later = [(jnp.add, perms[1]), (join, perms[0]), (join, core)]

    def step_b():
        f, perm = later.pop(0)
        state["b"] = then(f, state["b"], state["rb"])
        state["rb"] = lax.ppermute(state["b"], "cols", perm)
        state["pb"] = (state["b"], state["rb"])

    gram_stages = xor_stages(jnp.add, "rows", n_rows) + [(join, "cols", core)]
    norm_stages = xor_stages(jnp.add, "cols", n_cols)
    sizes = [CHUNK] * (width // CHUNK)
    z = lax.axis_index("rows")
    ends = (z == 0) | (z == n_rows - 1)
    outer = [(i, i ^ 1) for i in range(n_rows)]
    inner = [(1, 2), (2, 1)]

    def raw(half):
        out = then(lambda *x: raw_call(*x, sizes), *state["p" + half], hi, lo)
        for i, piece in enumerate(out):
            state[f"{half}{i}"] = piece

    def gram():
        if "gram" in state:
            state["gram"].step()
        else:
            x = then(lambda m, *p: gram_call(m, p[:2], p[2:]), me.reshape(1), *pa, *state["pb"])
            state["gram"] = Sent(then, gram_stages, x)
        if not state["gram"].stages:
            x = state["gram"].x
            chips = [[(j, j ^ m) for j in range(n_cols)] for m in range(2, n_cols, 2)]
            state["pairs"] = [x] + [lax.ppermute(x, "cols", perm) for perm in chips]

    def factor():
        prev = [] if state["inv"] is None else [state["inv"]]
        n = len(state["pairs"])
        state["inv"] = then(lambda o, *g: chol_call(o, g[:n], *(g[n:] or [None])), xor_order, *state["pairs"], *prev)

    def basis():
        state["basis"] = then(lambda i, *p: basis_call(i, p[:2], p[2:]), state["inv"], *pa, *state["pb"])

    def send_outer(new, old):
        both = [state[k] for k in (new, old) if k]
        x = then(lambda *p: jnp.where(ends, p[0], p[-1]) if len(p) > 1 else p[0], *both)
        state["outer"] = (new, old, lax.ppermute(x, "rows", outer))

    def take_outer():
        new, old, r = state["outer"]
        if new:
            state[new] = then(lambda x, r: jnp.where(ends, x, x + r), state[new], r)
        if old:
            state[old] = then(lambda x, r: jnp.where(ends, r, x), state[old], r)

    def send_inner(k):
        state["inner"] = (k, lax.ppermute(state[k], "rows", inner))

    def take_inner():
        k, r = state["inner"]
        state[k] = then(jnp.add, state[k], r)

    state["pa"] = pa
    names = [f"{half}{i}" for half in "ab" for i in range(len(sizes))]
    parts = names + [None, None]

    count = iter(range(len(parts)))

    def take():
        if "outer" in state:
            take_outer()
            del state["outer"]
        if "inner" in state:
            take_inner()
            del state["inner"]

    def slot():
        take()
        k = next(count)
        send_outer(parts[k], names[k - 2] if k > 1 else None)
        if 0 < k <= len(names):
            send_inner(names[k - 1])

    steps = {"raw_a": lambda: raw("a"), "raw_b": lambda: raw("b"), "b": step_b, "gram": gram}
    steps |= {"factor": factor, "basis": basis, "slot": slot, "take": take}
    for name in SCHEDULE:
        steps[name]()
    inv, (bh, bl) = state["inv"], state["basis"]
    raws = [state[name] for name in names]
    cross, ch, cl, sq = then(lambda i, *r: cross_call(i, r, 0), inv, *raws)
    norm = Sent(then, norm_stages, sq)
    norm.step()
    part = then(lambda *x: momentum_call(*x, 0, None), order, bh, bl, hi, lo, ch, cl)
    norm.step()
    momentum_next = then(lambda p, *x: momentum_call(*x, n_cols // 2, p), part, order, bh, bl, hi, lo, ch, cl)
    scale = momentum_prev.shape[0] * n_rows / rank**0.5
    update, q_next = then(lambda *x: update_call(*x, scale), order, bh, bl, cross, ch, cl, norm.finish())
    return momentum_next, q_next, update


def plain(n_rows, n_cols, momentum_prev, gradient, q_prev):
    high = lax.Precision.HIGHEST
    dot = functools.partial(lax.dot_general, precision=high, preferred_element_type=F32)
    momentum = 0.95 * momentum_prev + gradient.astype(F32)
    power = lax.psum_scatter(dot(momentum, q_prev, NN), "cols", scatter_dimension=0, tiled=True)
    power = lax.all_gather(power, "cols", axis=0, tiled=True)
    tn = (((0,), (0,)), ((), ()))
    raw, gram = lax.psum((dot(momentum, power, tn), dot(power, power, tn)), "rows")
    chol = jnp.linalg.cholesky(gram)
    solve = functools.partial(lax.linalg.triangular_solve, chol, left_side=False, lower=True, transpose_a=True)
    basis, cross = solve(power), solve(raw)
    q_next = cross / (jnp.sqrt(lax.psum(jnp.sum(cross * cross, axis=0), "cols")) + 1e-08)
    momentum_next = momentum - 0.5 * dot(basis, cross, NT)
    factor = momentum_prev.shape[0] * n_rows / jnp.sqrt(jnp.float32(q_prev.shape[1]))
    return momentum_next, q_next, (factor * dot(basis, q_next, NT)).astype(BF16)


def solution(mesh):
    n_rows, n_cols = mesh.shape["rows"], mesh.shape["cols"]

    def body(momentum_prev, gradient, q_prev):
        rows, cols = momentum_prev.shape
        block = rows // n_cols
        fits = (
            n_rows == 4
            and n_cols == 8
            and block % 128 == 0
            and cols % 128 == 0
            and q_prev.shape[1] % (4 * CHUNK) == 0
        )
        return (fast if fits else plain)(n_rows, n_cols, momentum_prev, gradient, q_prev)

    in_specs = (P("rows", "cols"), P("rows", "cols"), P("cols", None))
    out_specs = (P("rows", "cols"), P("cols", None), P("rows", "cols"))
    return jax.shard_map(body, mesh=mesh, in_specs=in_specs, out_specs=out_specs, check_vma=False)
```

```python
import functools

import jax
import jax.numpy as jnp
from jax import lax
from jax.experimental import pallas as pl
from jax.experimental.pallas import tpu as pltpu
from jax.sharding import PartitionSpec as P

CHUNK = 128
SHRINK = 1
PANEL = 8
SCHEDULE = [
    *["raw_a", "slot", "b", "b", "slot", "b", "gram", "raw_b", "gram", "slot", "gram", "gram", "factor"],
    *["slot", "factor", "slot", "factor", "slot", "factor", "basis", "take"],
]
F32, BF16 = jnp.float32, jnp.bfloat16
HIGHEST = lax.Precision.HIGHEST
NN = (((1,), (0,)), ((), ()))
NT = (((1,), (1,)), ((), ()))
MIB = 1024 * 1024
VMEM = pl.BlockSpec(memory_space=pltpu.VMEM)
SMEM = pl.BlockSpec(memory_space=pltpu.SMEM)
HBM = pl.BlockSpec(memory_space=pltpu.HBM)
DMA = pltpu.SemaphoreType.DMA


def params(mib):
    return pltpu.CompilerParams(vmem_limit_bytes=mib * MIB)


def shape(dims, dtype=F32):
    return jax.ShapeDtypeStruct(dims, dtype)


def cost(flops, nbytes):
    return pl.CostEstimate(flops=int(flops) // SHRINK, bytes_accessed=int(nbytes) // SHRINK, transcendentals=0)


def split(x):
    hi = x.astype(BF16)
    return hi, (x - hi.astype(F32)).astype(BF16)


def dot1(a, b, dims):
    return lax.dot_general(a, b, dims, preferred_element_type=F32)


def dot3(ah, al, bh, bl, dims=NN):
    return dot1(ah, bh, dims) + (dot1(al, bh, dims) + dot1(ah, bl, dims))


def dot_high(a, b, dims):
    return lax.dot_general(a, b, dims, precision=HIGHEST, preferred_element_type=F32)


def bit_orders(bits):
    rest = list(range(1, bits))
    half = (len(rest) + 1) // 2
    return rest, rest[half:] + rest[:half]


def position_masks(bits, parity):
    orders = bit_orders(bits)

    def walk(order):
        masks = [0]
        for bit in reversed(order):
            masks = masks + [m ^ (1 << bit) for m in masks]
        return masks

    return walk(orders[parity]) + [1 ^ m for m in walk(orders[1 - parity])]


def pair_perms(bits):
    orders = bit_orders(bits)
    n = 1 << bits
    return [[(j, j ^ (1 << orders[j & 1][step])) for j in range(n)] for step in range(bits - 1)]


class Order:
    def __init__(self):
        self.token = None

    def __call__(self, f, *args):
        if self.token is not None:
            args, _ = lax.optimization_barrier((args, self.token))
        out = f(*args)
        self.token = jax.tree.leaves(out)[0]
        return out


def in_hbm(*xs):
    return [pltpu.with_memory_space_constraint(x, pltpu.HBM) for x in xs]


def in_vmem(*xs):
    return [pltpu.with_memory_space_constraint(x, pltpu.VMEM) for x in xs]


class Sent:
    def __init__(self, then, stages, x):
        self.then, self.stages = then, list(stages)
        self.send(x)

    def send(self, x):
        self.x = x
        if self.stages:
            self.received = lax.ppermute(x, *self.stages[0][1:])

    def step(self):
        if not self.stages:
            return
        combine = self.stages.pop(0)[0]
        self.send(self.then(combine, self.x, self.received))

    def finish(self):
        while self.stages:
            self.step()
        return self.x


def join(x, r):
    return jnp.concatenate([x, r], axis=0)


def xor_stages(combine, axis, n):
    bits = range(n.bit_length() - 1)
    return [(combine, axis, [(i, i ^ (1 << bit)) for i in range(n)]) for bit in bits]


def first_kernel(order_ref, mp_ref, g_ref, q_ref, hi_ref, lo_ref, keep_ref, send_ref, mb, gb, qb, qs, sm, sg, sq):
    half, width, block = keep_ref.shape

    def copies(t):
        rows = pl.ds(pl.multiple_of(order_ref[t] * block, block), block)
        return [
            pltpu.make_async_copy(mp_ref.at[rows, :], mb.at[t], sm.at[t]),
            pltpu.make_async_copy(g_ref.at[rows, :], gb.at[t], sg.at[t]),
        ]

    q_copy = pltpu.make_async_copy(q_ref, qb, sq)
    q_copy.start()
    for t in range(2 * half):
        for copy in copies(t):
            copy.start()
    q_copy.wait()
    qs[:, :width], qs[:, width:] = split(qb[:, :width])

    def part(out_ref, first, t):
        for copy in copies(first + t):
            copy.wait()
        h, l = split(0.95 * mb[first + t] + gb[first + t].astype(F32))
        rows = pl.ds(pl.multiple_of((first + t) * block, block), block)
        hi_ref[rows, :] = h
        lo_ref[rows, :] = l
        both = dot1(h, qs[...], NN)
        out_ref[t] = (both[:, :width] + (both[:, width:] + dot1(l, qs[:, :width], NN))).T

    for first, out_ref in ((0, keep_ref), (half, send_ref)):
        lax.fori_loop(0, half, lambda t, _: part(out_ref, first, t), None)


def first_call(order, mp, g, q, width):
    rows, cols = mp.shape
    blocks = order.shape[0]
    block, half = rows // blocks, blocks // 2
    return pl.pallas_call(
        first_kernel,
        in_specs=[SMEM, HBM, HBM, HBM],
        out_specs=[VMEM] * 4,
        out_shape=[pltpu.VMEM((rows, cols), BF16)] * 2 + [shape((half, width, block))] * 2,
        scratch_shapes=[
            pltpu.VMEM((blocks, block, cols), F32),
            pltpu.VMEM((blocks, block, cols), BF16),
            pltpu.VMEM(q.shape, F32),
            pltpu.VMEM((cols, 2 * width), BF16),
            DMA((blocks,)),
            DMA((blocks,)),
            DMA,
        ],
        compiler_params=params(26),
        cost_estimate=cost(6 * rows * cols * width, 6 * rows * cols),
        name="momentum_and_power",
    )(order, *in_hbm(mp, g, q))


def rest_kernel(hi_ref, lo_ref, q_ref, keep_ref, send_ref, qb, sem):
    half, width, block = keep_ref.shape
    copy = pltpu.make_async_copy(q_ref, qb, sem)
    copy.start()
    copy.wait()
    qh, ql = split(qb[:, qb.shape[1] - width :])
    for t in range(2 * half):
        rows = slice(t * block, (t + 1) * block)
        out_ref = keep_ref if t < half else send_ref
        out_ref[t % half] = dot3(hi_ref[rows, :], lo_ref[rows, :], qh, ql).T


def rest_call(hi, lo, q, width, blocks):
    rows, cols = hi.shape
    block, half = rows // blocks, blocks // 2
    return pl.pallas_call(
        rest_kernel,
        in_specs=[VMEM, VMEM, HBM],
        out_specs=[VMEM] * 2,
        out_shape=[shape((half, width, block))] * 2,
        scratch_shapes=[pltpu.VMEM(q.shape, F32), DMA],
        compiler_params=params(16),
        cost_estimate=cost(6 * rows * cols * width, 4 * rows * cols),
        name="power",
    )(*in_vmem(hi, lo), *in_hbm(q))


def block_at(pieces, t):
    per = pieces[0].shape[0]
    return pieces[t // per].at[t % per]


def raw_kernel(n, *refs):
    pieces, (hi_ref, lo_ref), outs, acc = refs[:n], refs[n : n + 2], refs[n + 2 : -1], refs[-1]
    per, width, block = pieces[0].shape
    for t in range(n * per):
        ph, plo = split(block_at(pieces, t)[...])
        rows = slice(t * block, (t + 1) * block)
        both = dot1(jnp.concatenate([ph, plo], axis=0), hi_ref[rows, :], NN)
        term = both[:width] + (both[width:] + dot1(ph, lo_ref[rows, :], NN))
        acc[...] = term if t == 0 else acc[...] + term
    off = 0
    for out in outs:
        out[...] = acc[off : off + out.shape[0]]
        off += out.shape[0]


def raw_call(pieces, hi, lo, parts):
    rows, cols = hi.shape
    width = sum(parts)
    return pl.pallas_call(
        functools.partial(raw_kernel, len(pieces)),
        in_specs=[VMEM] * (len(pieces) + 2),
        out_specs=[VMEM] * len(parts),
        out_shape=[shape((p, cols)) for p in parts],
        scratch_shapes=[pltpu.VMEM((width, cols), F32)],
        compiler_params=params(16),
        cost_estimate=cost(6 * rows * cols * width, 4 * rows * cols),
        name="raw",
    )(*pieces, *in_vmem(hi, lo))


def split3(x):
    hi, lo = split(x)
    return hi, lo, (x - hi.astype(F32) - lo.astype(F32)).astype(BF16)


def gram_kernel(n_first, me_ref, *refs):
    first, last, out_ref = refs[:n_first], refs[n_first:-1], refs[-1]
    per, width, _ = first[0].shape
    n = out_ref.shape[0]
    mine = pl.ds(pl.multiple_of(me_ref[0] * n, n), n)
    sums = None
    for t in range(n_first * per):
        refs = [block_at(first, t), block_at(last, t)]
        x1, x2, x3 = split3(jnp.concatenate([r[...] for r in refs], axis=0))
        y = jnp.concatenate([r[mine, :] for r in refs], axis=0)
        y = jnp.concatenate(split3(y), axis=0)
        terms = [dot1(x1, y, NT), dot1(x2, y[: 4 * n], NT), dot1(x3, y[: 2 * n], NT)]
        sums = terms if sums is None else [s + u for s, u in zip(sums, terms)]
    z1, z2, z3 = sums
    n = 2 * n
    small = z1[:, 2 * n :] + (z2[:, n:] + z3)
    rows = (z1[:, :n] + ((z1[:, n : 2 * n] + z2[:, :n]) + small)).T
    out_ref[:, : 2 * width] = rows[n // 2 :]
    out_ref[:, 2 * width :] = rows[: n // 2, :width]


def gram_call(me, pa, pb):
    refs = [*pa, *pb]
    blocks = len(pa) * pa[0].shape[0]
    _, width, block = pa[0].shape
    return pl.pallas_call(
        functools.partial(gram_kernel, len(pa)),
        in_specs=[SMEM] + [VMEM] * len(refs),
        out_specs=VMEM,
        out_shape=shape((width // blocks, 3 * width)),
        compiler_params=params(16),
        cost_estimate=cost(4e9, 16 * blocks * block * width),
        name="gram",
    )(me, *refs)


def eliminate(s_ref, w_ref):
    n = s_ref.shape[0]
    row = lax.broadcasted_iota(jnp.int32, (n, n), 0)
    col = lax.broadcasted_iota(jnp.int32, (n, n), 1)
    w_ref[...] = (row == col).astype(F32)
    full = (PANEL, n)
    sub = lax.broadcasted_iota(jnp.int32, full, 0)
    for base in range(0, n, PANEL):
        panel = s_ref[base : base + PANEL, :]
        wpanel = w_ref[base : base + PANEL, :]
        rows = [jnp.broadcast_to(panel[i : i + 1, :], full) for i in range(PANEL)]
        wrows = [jnp.broadcast_to(wpanel[i : i + 1, :], full) for i in range(PANEL)]
        v = {}
        for i in range(PANEL):
            for k in range(i, PANEL):
                v[i, k] = jnp.broadcast_to(rows[i][:, base + k : base + k + 1], full)
        mult, inv = {}, []
        for i in range(PANEL):
            r = 1.0 / v[i, i]
            inv.append(r)
            for a in range(i + 1, PANEL):
                m = v[i, a] * r
                mult[i, a] = m
                for k in range(a, PANEL):
                    v[a, k] = v[a, k] - m * v[i, k]
                rows[a] = rows[a] - m * rows[i]
                wrows[a] = wrows[a] - m * wrows[i]
        out = wrows[0] * lax.rsqrt(v[0, 0])
        for i in range(1, PANEL):
            out = jnp.where(sub == i, wrows[i] * lax.rsqrt(v[i, i]), out)
        w_ref[base : base + PANEL, :] = out
        for below in range(base + PANEL, n, PANEL):
            s = s_ref[below : below + PANEL, :]
            w = w_ref[below : below + PANEL, :]
            f = [jnp.broadcast_to(s[:, base + i : base + i + 1], full) for i in range(PANEL)]
            for i in range(PANEL):
                for a in range(i + 1, PANEL):
                    f[a] = f[a] - mult[i, a] * f[i]
            for i in range(PANEL):
                g = f[i] * inv[i]
                s = s - g * rows[i]
                w = w - g * wrows[i]
            s_ref[below : below + PANEL, :] = s
            w_ref[below : below + PANEL, :] = w


def chol_kernel(base, n_pairs, order_ref, *refs):
    pairs, refs = refs[:n_pairs], refs[n_pairs:]
    prev = refs[0] if base else None
    out_ref, g_ref, s_ref, w_ref = refs[1 if base else 0 :]
    rows, width = pairs[0].shape[0] // 2, pairs[0].shape[1] // 3
    here, end = slice(base, base + CHUNK), base + CHUNK
    lanes = slice(0, end) if base >= width else slice(2 * width, 2 * width + end)
    for i in range(CHUNK // rows):
        mask = order_ref[base // rows % (2 * n_pairs) + i]
        local = pl.ds(pl.multiple_of(mask % 2 * rows, rows), rows)
        piece = pairs[0][local, lanes]
        for p in range(1, n_pairs):
            piece = jnp.where(mask // 2 == p, pairs[p][local, lanes], piece)
        g_ref[i * rows : (i + 1) * rows, :] = piece
    s = g_ref[:, here]
    if base:
        before = prev[...]
        lrow = dot_high(g_ref[:, :base], before, NT)
        s = s - dot_high(lrow, lrow, NT)
    s_ref[...] = s
    eliminate(s_ref, w_ref)
    w = w_ref[...]
    out_ref[here, here] = w
    if base:
        out_ref[:base, :base] = before
        out_ref[:base, here] = jnp.zeros((base, CHUNK), F32)
        out_ref[here, :base] = -dot_high(w, dot_high(lrow, before, NN), NN)


def chol_call(order, pairs, prev):
    base = prev.shape[0] if prev is not None else 0
    size = base + CHUNK
    args = list(pairs) + ([prev] if base else [])
    return pl.pallas_call(
        functools.partial(chol_kernel, base, len(pairs)),
        in_specs=[SMEM] + [VMEM] * len(args),
        out_specs=VMEM,
        out_shape=shape((size, size)),
        scratch_shapes=[pltpu.VMEM((CHUNK, size), F32)] + [pltpu.VMEM((CHUNK, CHUNK), F32)] * 2,
        compiler_params=params(8),
        cost_estimate=cost(6e9, 8 * size * size),
        name="chol",
    )(order, *args)


def basis_kernel(n_first, inv_ref, *refs):
    first, last, (bh_ref, bl_ref) = refs[:n_first], refs[n_first:-2], refs[-2:]
    per, _, block = first[0].shape
    ih, il = split(inv_ref[...])
    for t in range(n_first * per):
        ph, plo = split(jnp.concatenate([block_at(first, t)[...], block_at(last, t)[...]], axis=0))
        rows = slice(t * block, (t + 1) * block)
        bh_ref[rows, :], bl_ref[rows, :] = split(dot3(ih, il, ph, plo).T)


def basis_call(inv, pa, pb):
    refs = [*pa, *pb]
    blocks = len(pa) * pa[0].shape[0]
    _, width, block = pa[0].shape
    return pl.pallas_call(
        functools.partial(basis_kernel, len(pa)),
        in_specs=[VMEM] * (1 + len(refs)),
        out_specs=[VMEM, VMEM],
        out_shape=[pltpu.VMEM((blocks * block, 2 * width), BF16)] * 2,
        compiler_params=params(16),
        cost_estimate=cost(24 * width * width * block * blocks, 16 * width * block * blocks),
        name="basis",
    )(inv, *refs)


def cross_kernel(skip, inv_ref, *refs):
    raws, (out_ref, ch_ref, cl_ref, sq_ref) = refs[:-4], refs[-4:]
    size = skip + out_ref.shape[0]
    ih, il = split(inv_ref[skip:size, :size])
    rh, rl = split(jnp.concatenate([r[...] for r in raws], axis=0))
    cross = dot3(ih, il, rh, rl)
    out_ref[...] = cross
    ch_ref[...], cl_ref[...] = split(cross)
    sq_ref[...] = jnp.sum(cross * cross, axis=1, keepdims=True).T


def cross_call(inv, raws, skip):
    cols = raws[0].shape[1]
    rows = sum(r.shape[0] for r in raws) - skip
    return pl.pallas_call(
        functools.partial(cross_kernel, skip),
        in_specs=[VMEM] * (1 + len(raws)),
        out_specs=[VMEM] * 4,
        out_shape=[pltpu.VMEM((rows, cols), F32), pltpu.VMEM((rows, cols), BF16), pltpu.VMEM((rows, cols), BF16), shape((1, rows))],
        compiler_params=params(16),
        cost_estimate=cost(6 * rows * (rows + skip) * cols, 8 * rows * cols),
        name="cross",
    )(inv, *raws)


def store_rows(order_ref, place, buf, t, out_ref, sem):
    block = buf.shape[1]
    rows = pl.ds(pl.multiple_of(order_ref[place] * block, block), block)
    copy = pltpu.make_async_copy(buf.at[t], out_ref.at[rows, :], sem.at[t])
    copy.start()
    return copy


def momentum_kernel(first, order_ref, bh_ref, bl_ref, hi_ref, lo_ref, ch_ref, cl_ref, *refs):
    out_ref, buf, sem = refs[-3:]
    blocks, block, _ = buf.shape
    copies = []
    for t in range(blocks):
        rows = slice((first + t) * block, (first + t + 1) * block)
        prod = dot3(bh_ref[rows, :], bl_ref[rows, :], ch_ref[...], cl_ref[...])
        buf[t] = (hi_ref[rows, :].astype(F32) + lo_ref[rows, :].astype(F32)) - 0.5 * prod
        copies.append(store_rows(order_ref, first + t, buf, t, out_ref, sem))
    for copy in copies:
        copy.wait()


def momentum_call(order, bh, bl, hi, lo, ch, cl, first, so_far):
    rows, cols = hi.shape
    rank, blocks = bh.shape[1], order.shape[0]
    more = [] if so_far is None else [so_far]
    args = in_vmem(bh, bl, hi, lo, ch, cl)
    return pl.pallas_call(
        functools.partial(momentum_kernel, first),
        in_specs=[SMEM] + [VMEM] * len(args) + [HBM] * len(more),
        out_specs=HBM,
        out_shape=shape((rows, cols)),
        scratch_shapes=[pltpu.VMEM((blocks // 2, rows // blocks, cols), F32), DMA((blocks // 2,))],
        input_output_aliases={1 + len(args): 0} if more else {},
        compiler_params=params(12),
        cost_estimate=cost(3 * rows * cols * rank, 4 * rows * cols),
        name="momentum_next",
    )(order, *args, *more)


def update_kernel(factor, order_ref, bh_ref, bl_ref, c_ref, ch_ref, cl_ref, sq_ref, out_ref, qn_ref, buf, qbuf, sem, qsem):
    blocks, block, cols = buf.shape
    scale = 1.0 / (jnp.sqrt(sq_ref[...]) + 1e-08)
    copies = []
    step = cols // blocks
    for t in range(blocks):
        rows = slice(t * block, (t + 1) * block)
        bh, bl = split((bh_ref[rows, :].astype(F32) + bl_ref[rows, :].astype(F32)) * scale)
        prod = dot3(bh, bl, ch_ref[...], cl_ref[...])
        buf[t] = (factor * prod).astype(BF16)
        copies.append(store_rows(order_ref, t, buf, t, out_ref, sem))
        qbuf[t] = c_ref[:, t * step : (t + 1) * step].T * scale
        copy = pltpu.make_async_copy(qbuf.at[t], qn_ref.at[pl.ds(t * step, step), :], qsem.at[t])
        copy.start()
        copies.append(copy)
    for copy in copies:
        copy.wait()


def update_call(order, bh, bl, cross, ch, cl, sq, factor):
    rows, rank = bh.shape
    cols, blocks = cross.shape[1], order.shape[0]
    return pl.pallas_call(
        functools.partial(update_kernel, factor),
        in_specs=[SMEM] + [VMEM] * 6,
        out_specs=[HBM, HBM],
        out_shape=[shape((rows, cols), BF16), shape((cols, rank))],
        scratch_shapes=[
            pltpu.VMEM((blocks, rows // blocks, cols), BF16),
            pltpu.VMEM((blocks, cols // blocks, rank), F32),
            DMA((blocks,)),
            DMA((blocks,)),
        ],
        compiler_params=params(16),
        cost_estimate=cost(6 * rows * cols * rank, 8 * rows * cols),
        name="update",
    )(order, *in_vmem(bh, bl, cross, ch, cl), sq)


def fast(n_rows, n_cols, momentum_prev, gradient, q_prev):
    rank = q_prev.shape[1]
    width = rank // 2
    bits = n_cols.bit_length() - 1
    me = lax.axis_index("cols").astype(jnp.int32)
    masks = jnp.where(
        me % 2 == 0,
        jnp.array(position_masks(bits, 0), jnp.int32),
        jnp.array(position_masks(bits, 1), jnp.int32),
    )
    order = me ^ masks
    xor_order = me ^ jnp.arange(n_cols, dtype=jnp.int32)
    core = [(j, j ^ 1) for j in range(n_cols)]
    perms = pair_perms(bits)
    then = Order()

    def halve(k, r):
        n = k.shape[0] // 2
        return k[n:] + r[n:], k[:n] + r[:n]

    hi, lo, keep, send = then(lambda *x: first_call(*x, width), order, momentum_prev, gradient, q_prev)
    s, a = then(halve, keep, lax.ppermute(send, "cols", core))
    ra = lax.ppermute(s, "cols", perms[0])
    keep, send = then(lambda *x: rest_call(*x, rank - width, n_cols), hi, lo, q_prev)
    rb = lax.ppermute(send, "cols", core)
    s, a = then(halve, a, ra)
    a = then(jnp.add, a, lax.ppermute(s, "cols", perms[1]))
    ra = lax.ppermute(a, "cols", perms[1])

    def both_steps(a, ra, b, rb):
        s, b = halve(b, rb)
        a = join(a, ra)
        return join(a, s), a, b

    s, a, b = then(both_steps, a, ra, keep, rb)
    s = lax.ppermute(s, "cols", perms[0])
    n = a.shape[0]
    a = then(lambda a, s: join(a, s[:n]), a, s)
    pa = (a, lax.ppermute(a, "cols", core))
    s, b = then(halve, b, s[n:])
    state = {"inv": None, "b": b, "rb": lax.ppermute(s, "cols", perms[1])}
    later = [(jnp.add, perms[1]), (join, perms[0])]

    def step_b():
        if later:
            f, perm = later.pop(0)
            state["b"] = then(f, state["b"], state["rb"])
            state["rb"] = lax.ppermute(state["b"], "cols", perm)
        else:
            own = [state["b"], then(lambda r: r, state["rb"])]
            state["pb"] = (*own, *[lax.ppermute(x, "cols", core) for x in own])

    gram_stages = xor_stages(jnp.add, "rows", n_rows) + [(join, "cols", core)]
    norm_stages = xor_stages(jnp.add, "cols", n_cols)
    sizes = [CHUNK] * (width // CHUNK)
    z = lax.axis_index("rows")
    ends = (z == 0) | (z == n_rows - 1)
    outer = [(i, i ^ 1) for i in range(n_rows)]
    inner = [(1, 2), (2, 1)]

    def raw(half):
        out = then(lambda p, h, l: raw_call(p, h, l, sizes), state["p" + half], hi, lo)
        for i, piece in enumerate(out):
            state[f"{half}{i}"] = piece

    def gram():
        if "gram" in state:
            state["gram"].step()
        else:
            x = then(gram_call, me.reshape(1), pa, state["pb"])
            state["gram"] = Sent(then, gram_stages, x)
        if not state["gram"].stages:
            x = state["gram"].x
            chips = [[(j, j ^ m) for j in range(n_cols)] for m in range(2, n_cols, 2)]
            state["pairs"] = [x] + [lax.ppermute(x, "cols", perm) for perm in chips]

    def factor():
        prev = [] if state["inv"] is None else [state["inv"]]
        n = len(state["pairs"])
        state["inv"] = then(lambda o, *g: chol_call(o, g[:n], *(g[n:] or [None])), xor_order, *state["pairs"], *prev)

    def basis():
        state["basis"] = then(basis_call, state["inv"], pa, state["pb"])

    def send_outer(new, old):
        both = [state[k] for k in (new, old) if k]
        x = then(lambda *p: jnp.where(ends, p[0], p[-1]) if len(p) > 1 else p[0], *both)
        state["outer"] = (new, old, lax.ppermute(x, "rows", outer))

    def take_outer():
        new, old, r = state["outer"]
        if new:
            state[new] = then(lambda x, r: jnp.where(ends, x, x + r), state[new], r)
        if old:
            state[old] = then(lambda x, r: jnp.where(ends, r, x), state[old], r)

    def send_inner(k):
        state["inner"] = (k, lax.ppermute(state[k], "rows", inner))

    def take_inner():
        k, r = state["inner"]
        state[k] = then(jnp.add, state[k], r)

    state["pa"] = pa
    names = [f"{half}{i}" for half in "ab" for i in range(len(sizes))]
    parts = names + [None, None]

    count = iter(range(len(parts)))

    def take():
        if "outer" in state:
            take_outer()
            del state["outer"]
        if "inner" in state:
            take_inner()
            del state["inner"]

    def slot():
        take()
        k = next(count)
        send_outer(parts[k], names[k - 2] if k > 1 else None)
        if 0 < k <= len(names):
            send_inner(names[k - 1])

    steps = {"raw_a": lambda: raw("a"), "raw_b": lambda: raw("b"), "b": step_b, "gram": gram}
    steps |= {"factor": factor, "basis": basis, "slot": slot, "take": take}
    for name in SCHEDULE:
        steps[name]()
    inv, (bh, bl) = state["inv"], state["basis"]
    raws = [state[name] for name in names]
    cross, ch, cl, sq = then(lambda i, *r: cross_call(i, r, 0), inv, *raws)
    norm = Sent(then, norm_stages, sq)
    norm.step()
    part = then(lambda *x: momentum_call(*x, 0, None), order, bh, bl, hi, lo, ch, cl)
    norm.step()
    momentum_next = then(lambda p, *x: momentum_call(*x, n_cols // 2, p), part, order, bh, bl, hi, lo, ch, cl)
    scale = momentum_prev.shape[0] * n_rows / rank**0.5
    update, q_next = then(lambda *x: update_call(*x, scale), order, bh, bl, cross, ch, cl, norm.finish())
    return momentum_next, q_next, update


def plain(n_rows, n_cols, momentum_prev, gradient, q_prev):
    high = lax.Precision.HIGHEST
    dot = functools.partial(lax.dot_general, precision=high, preferred_element_type=F32)
    momentum = 0.95 * momentum_prev + gradient.astype(F32)
    power = lax.psum_scatter(dot(momentum, q_prev, NN), "cols", scatter_dimension=0, tiled=True)
    power = lax.all_gather(power, "cols", axis=0, tiled=True)
    tn = (((0,), (0,)), ((), ()))
    raw, gram = lax.psum((dot(momentum, power, tn), dot(power, power, tn)), "rows")
    chol = jnp.linalg.cholesky(gram)
    solve = functools.partial(lax.linalg.triangular_solve, chol, left_side=False, lower=True, transpose_a=True)
    basis, cross = solve(power), solve(raw)
    q_next = cross / (jnp.sqrt(lax.psum(jnp.sum(cross * cross, axis=0), "cols")) + 1e-08)
    momentum_next = momentum - 0.5 * dot(basis, cross, NT)
    factor = momentum_prev.shape[0] * n_rows / jnp.sqrt(jnp.float32(q_prev.shape[1]))
    return momentum_next, q_next, (factor * dot(basis, q_next, NT)).astype(BF16)


def solution(mesh):
    n_rows, n_cols = mesh.shape["rows"], mesh.shape["cols"]

    def body(momentum_prev, gradient, q_prev):
        rows, cols = momentum_prev.shape
        block = rows // n_cols
        fits = (
            n_rows == 4
            and n_cols == 8
            and block % 128 == 0
            and cols % 128 == 0
            and q_prev.shape[1] % (4 * CHUNK) == 0
        )
        return (fast if fits else plain)(n_rows, n_cols, momentum_prev, gradient, q_prev)

    in_specs = (P("rows", "cols"), P("rows", "cols"), P("cols", None))
    out_specs = (P("rows", "cols"), P("cols", None), P("rows", "cols"))
    return jax.shard_map(body, mesh=mesh, in_specs=in_specs, out_specs=out_specs, check_vma=False)
```

```python
import functools

import jax
import jax.numpy as jnp
from jax import lax
from jax.experimental import pallas as pl
from jax.experimental.pallas import tpu as pltpu
from jax.sharding import PartitionSpec as P

CHUNK = 128
SHRINK = 1
PANEL = 8
SCHEDULE = [
    *["raw_a", "slot", "b", "b", "slot", "b", "gram", "raw_b", "gram", "slot", "gram", "gram", "factor"],
    *["slot", "factor", "slot", "factor", "slot", "factor", "basis", "take"],
]
F32, BF16 = jnp.float32, jnp.bfloat16
HIGHEST = lax.Precision.HIGHEST
NN = (((1,), (0,)), ((), ()))
NT = (((1,), (1,)), ((), ()))
MIB = 1024 * 1024
VMEM = pl.BlockSpec(memory_space=pltpu.VMEM)
SMEM = pl.BlockSpec(memory_space=pltpu.SMEM)
HBM = pl.BlockSpec(memory_space=pltpu.HBM)
DMA = pltpu.SemaphoreType.DMA


def params(mib):
    return pltpu.CompilerParams(vmem_limit_bytes=mib * MIB)


def shape(dims, dtype=F32):
    return jax.ShapeDtypeStruct(dims, dtype)


def cost(flops, nbytes):
    return pl.CostEstimate(flops=int(flops) // SHRINK, bytes_accessed=int(nbytes) // SHRINK, transcendentals=0)


def split(x):
    hi = x.astype(BF16)
    return hi, (x - hi.astype(F32)).astype(BF16)


def dot1(a, b, dims):
    return lax.dot_general(a, b, dims, preferred_element_type=F32)


def dot3(ah, al, bh, bl, dims=NN):
    return dot1(ah, bh, dims) + (dot1(al, bh, dims) + dot1(ah, bl, dims))


def dot_high(a, b, dims):
    return lax.dot_general(a, b, dims, precision=HIGHEST, preferred_element_type=F32)


def bit_orders(bits):
    rest = list(range(1, bits))
    half = (len(rest) + 1) // 2
    return rest, rest[half:] + rest[:half]


def position_masks(bits, parity):
    orders = bit_orders(bits)

    def walk(order):
        masks = [0]
        for bit in reversed(order):
            masks = masks + [m ^ (1 << bit) for m in masks]
        return masks

    return walk(orders[parity]) + [1 ^ m for m in walk(orders[1 - parity])]


def pair_perms(bits):
    orders = bit_orders(bits)
    n = 1 << bits
    return [[(j, j ^ (1 << orders[j & 1][step])) for j in range(n)] for step in range(bits - 1)]


class Order:
    def __init__(self):
        self.token = None

    def __call__(self, f, *args):
        if self.token is not None:
            args, _ = lax.optimization_barrier((args, self.token))
        out = f(*args)
        self.token = jax.tree.leaves(out)[0]
        return out


def in_hbm(*xs):
    return [pltpu.with_memory_space_constraint(x, pltpu.HBM) for x in xs]


def in_vmem(*xs):
    return [pltpu.with_memory_space_constraint(x, pltpu.VMEM) for x in xs]


class Sent:
    def __init__(self, then, stages, x):
        self.then, self.stages = then, list(stages)
        self.send(x)

    def send(self, x):
        self.x = x
        if self.stages:
            self.received = lax.ppermute(x, *self.stages[0][1:])

    def step(self):
        if not self.stages:
            return
        combine = self.stages.pop(0)[0]
        self.send(self.then(combine, self.x, self.received))

    def finish(self):
        while self.stages:
            self.step()
        return self.x


def join(x, r):
    return jnp.concatenate([x, r], axis=0)


def xor_stages(combine, axis, n):
    bits = range(n.bit_length() - 1)
    return [(combine, axis, [(i, i ^ (1 << bit)) for i in range(n)]) for bit in bits]


def first_kernel(order_ref, mp_ref, g_ref, q_ref, hi_ref, lo_ref, keep_ref, send_ref, mb, gb, qb, qs, sm, sg, sq):
    half, width, block = keep_ref.shape

    def copies(t):
        rows = pl.ds(pl.multiple_of(order_ref[t] * block, block), block)
        return [
            pltpu.make_async_copy(mp_ref.at[rows, :], mb.at[t], sm.at[t]),
            pltpu.make_async_copy(g_ref.at[rows, :], gb.at[t], sg.at[t]),
        ]

    q_copy = pltpu.make_async_copy(q_ref, qb, sq)
    q_copy.start()
    for t in range(2 * half):
        for copy in copies(t):
            copy.start()
    q_copy.wait()
    qs[:, :width], qs[:, width:] = split(qb[:, :width])

    def part(out_ref, first, t):
        for copy in copies(first + t):
            copy.wait()
        h, l = split(0.95 * mb[first + t] + gb[first + t].astype(F32))
        rows = pl.ds(pl.multiple_of((first + t) * block, block), block)
        hi_ref[rows, :] = h
        lo_ref[rows, :] = l
        both = dot1(h, qs[...], NN)
        out_ref[t] = (both[:, :width] + (both[:, width:] + dot1(l, qs[:, :width], NN))).T

    for first, out_ref in ((0, keep_ref), (half, send_ref)):
        lax.fori_loop(0, half, lambda t, _: part(out_ref, first, t), None)


def first_call(order, mp, g, q, width):
    rows, cols = mp.shape
    blocks = order.shape[0]
    block, half = rows // blocks, blocks // 2
    return pl.pallas_call(
        first_kernel,
        in_specs=[SMEM, HBM, HBM, HBM],
        out_specs=[VMEM] * 4,
        out_shape=[pltpu.VMEM((rows, cols), BF16)] * 2 + [shape((half, width, block))] * 2,
        scratch_shapes=[
            pltpu.VMEM((blocks, block, cols), F32),
            pltpu.VMEM((blocks, block, cols), BF16),
            pltpu.VMEM(q.shape, F32),
            pltpu.VMEM((cols, 2 * width), BF16),
            DMA((blocks,)),
            DMA((blocks,)),
            DMA,
        ],
        compiler_params=params(26),
        cost_estimate=cost(6 * rows * cols * width, 6 * rows * cols),
        name="momentum_and_power",
    )(order, *in_hbm(mp, g, q))


def rest_kernel(hi_ref, lo_ref, q_ref, keep_ref, send_ref, qb, sem):
    half, width, block = keep_ref.shape
    copy = pltpu.make_async_copy(q_ref, qb, sem)
    copy.start()
    copy.wait()
    qh, ql = split(qb[:, qb.shape[1] - width :])
    for t in range(2 * half):
        rows = slice(t * block, (t + 1) * block)
        out_ref = keep_ref if t < half else send_ref
        out_ref[t % half] = dot3(hi_ref[rows, :], lo_ref[rows, :], qh, ql).T


def rest_call(hi, lo, q, width, blocks):
    rows, cols = hi.shape
    block, half = rows // blocks, blocks // 2
    return pl.pallas_call(
        rest_kernel,
        in_specs=[VMEM, VMEM, HBM],
        out_specs=[VMEM] * 2,
        out_shape=[shape((half, width, block))] * 2,
        scratch_shapes=[pltpu.VMEM(q.shape, F32), DMA],
        compiler_params=params(16),
        cost_estimate=cost(6 * rows * cols * width, 4 * rows * cols),
        name="power",
    )(*in_vmem(hi, lo), *in_hbm(q))


def block_at(pieces, t):
    per = pieces[0].shape[0]
    return pieces[t // per].at[t % per]


def raw_kernel(n, *refs):
    pieces, (hi_ref, lo_ref), outs, acc = refs[:n], refs[n : n + 2], refs[n + 2 : -1], refs[-1]
    per, width, block = pieces[0].shape
    for t in range(n * per):
        ph, plo = split(block_at(pieces, t)[...])
        rows = slice(t * block, (t + 1) * block)
        both = dot1(jnp.concatenate([ph, plo], axis=0), hi_ref[rows, :], NN)
        term = both[:width] + (both[width:] + dot1(ph, lo_ref[rows, :], NN))
        acc[...] = term if t == 0 else acc[...] + term
    off = 0
    for out in outs:
        out[...] = acc[off : off + out.shape[0]]
        off += out.shape[0]


def raw_call(pieces, hi, lo, parts):
    rows, cols = hi.shape
    width = sum(parts)
    return pl.pallas_call(
        functools.partial(raw_kernel, len(pieces)),
        in_specs=[VMEM] * (len(pieces) + 2),
        out_specs=[VMEM] * len(parts),
        out_shape=[shape((p, cols)) for p in parts],
        scratch_shapes=[pltpu.VMEM((width, cols), F32)],
        compiler_params=params(16),
        cost_estimate=cost(6 * rows * cols * width, 4 * rows * cols),
        name="raw",
    )(*pieces, *in_vmem(hi, lo))


def split3(x):
    hi, lo = split(x)
    return hi, lo, (x - hi.astype(F32) - lo.astype(F32)).astype(BF16)


def gram_kernel(n_first, me_ref, *refs):
    first, last, out_ref = refs[:n_first], refs[n_first:-1], refs[-1]
    per, width, _ = first[0].shape
    n = out_ref.shape[0]
    mine = pl.ds(pl.multiple_of(me_ref[0] * n, n), n)
    sums = None
    for t in range(n_first * per):
        refs = [block_at(first, t), block_at(last, t)]
        x1, x2, x3 = split3(jnp.concatenate([r[...] for r in refs], axis=0))
        y = jnp.concatenate([r[mine, :] for r in refs], axis=0)
        y = jnp.concatenate(split3(y), axis=0)
        terms = [dot1(x1, y, NT), dot1(x2, y[: 4 * n], NT), dot1(x3, y[: 2 * n], NT)]
        sums = terms if sums is None else [s + u for s, u in zip(sums, terms)]
    z1, z2, z3 = sums
    n = 2 * n
    small = z1[:, 2 * n :] + (z2[:, n:] + z3)
    rows = (z1[:, :n] + ((z1[:, n : 2 * n] + z2[:, :n]) + small)).T
    out_ref[:, : 2 * width] = rows[n // 2 :]
    out_ref[:, 2 * width :] = rows[: n // 2, :width]


def gram_call(me, pa, pb):
    refs = [*pa, *pb]
    blocks = len(pa) * pa[0].shape[0]
    _, width, block = pa[0].shape
    return pl.pallas_call(
        functools.partial(gram_kernel, len(pa)),
        in_specs=[SMEM] + [VMEM] * len(refs),
        out_specs=VMEM,
        out_shape=shape((width // blocks, 3 * width)),
        compiler_params=params(16),
        cost_estimate=cost(4e9, 16 * blocks * block * width),
        name="gram",
    )(me, *refs)


def eliminate(s_ref, w_ref):
    n = s_ref.shape[0]
    row = lax.broadcasted_iota(jnp.int32, (n, n), 0)
    col = lax.broadcasted_iota(jnp.int32, (n, n), 1)
    w_ref[...] = (row == col).astype(F32)
    full = (PANEL, n)
    sub = lax.broadcasted_iota(jnp.int32, full, 0)
    for base in range(0, n, PANEL):
        panel = s_ref[base : base + PANEL, :]
        wpanel = w_ref[base : base + PANEL, :]
        rows = [jnp.broadcast_to(panel[i : i + 1, :], full) for i in range(PANEL)]
        wrows = [jnp.broadcast_to(wpanel[i : i + 1, :], full) for i in range(PANEL)]
        v = {}
        for i in range(PANEL):
            for k in range(i, PANEL):
                v[i, k] = jnp.broadcast_to(rows[i][:, base + k : base + k + 1], full)
        mult, inv = {}, []
        for i in range(PANEL):
            r = 1.0 / v[i, i]
            inv.append(r)
            for a in range(i + 1, PANEL):
                m = v[i, a] * r
                mult[i, a] = m
                for k in range(a, PANEL):
                    v[a, k] = v[a, k] - m * v[i, k]
                rows[a] = rows[a] - m * rows[i]
                wrows[a] = wrows[a] - m * wrows[i]
        out = wrows[0] * lax.rsqrt(v[0, 0])
        for i in range(1, PANEL):
            out = jnp.where(sub == i, wrows[i] * lax.rsqrt(v[i, i]), out)
        w_ref[base : base + PANEL, :] = out
        for below in range(base + PANEL, n, PANEL):
            s = s_ref[below : below + PANEL, :]
            w = w_ref[below : below + PANEL, :]
            f = [jnp.broadcast_to(s[:, base + i : base + i + 1], full) for i in range(PANEL)]
            for i in range(PANEL):
                for a in range(i + 1, PANEL):
                    f[a] = f[a] - mult[i, a] * f[i]
            for i in range(PANEL):
                g = f[i] * inv[i]
                s = s - g * rows[i]
                w = w - g * wrows[i]
            s_ref[below : below + PANEL, :] = s
            w_ref[below : below + PANEL, :] = w


def chol_kernel(base, n_pairs, order_ref, *refs):
    pairs, refs = refs[:n_pairs], refs[n_pairs:]
    prev = refs[0] if base else None
    out_ref, g_ref, s_ref, w_ref = refs[1 if base else 0 :]
    rows, width = pairs[0].shape[0] // 2, pairs[0].shape[1] // 3
    here, end = slice(base, base + CHUNK), base + CHUNK
    lanes = slice(0, end) if base >= width else slice(2 * width, 2 * width + end)
    for i in range(CHUNK // rows):
        mask = order_ref[base // rows % (2 * n_pairs) + i]
        local = pl.ds(pl.multiple_of(mask % 2 * rows, rows), rows)
        piece = pairs[0][local, lanes]
        for p in range(1, n_pairs):
            piece = jnp.where(mask // 2 == p, pairs[p][local, lanes], piece)
        g_ref[i * rows : (i + 1) * rows, :] = piece
    s = g_ref[:, here]
    if base:
        before = prev[...]
        lrow = dot_high(g_ref[:, :base], before, NT)
        s = s - dot_high(lrow, lrow, NT)
    s_ref[...] = s
    eliminate(s_ref, w_ref)
    w = w_ref[...]
    out_ref[here, here] = w
    if base:
        out_ref[:base, :base] = before
        out_ref[:base, here] = jnp.zeros((base, CHUNK), F32)
        out_ref[here, :base] = -dot_high(w, dot_high(lrow, before, NN), NN)


def chol_call(order, pairs, prev):
    base = prev.shape[0] if prev is not None else 0
    size = base + CHUNK
    args = list(pairs) + ([prev] if base else [])
    return pl.pallas_call(
        functools.partial(chol_kernel, base, len(pairs)),
        in_specs=[SMEM] + [VMEM] * len(args),
        out_specs=VMEM,
        out_shape=shape((size, size)),
        scratch_shapes=[pltpu.VMEM((CHUNK, size), F32)] + [pltpu.VMEM((CHUNK, CHUNK), F32)] * 2,
        compiler_params=params(8),
        cost_estimate=cost(6e9, 8 * size * size),
        name="chol",
    )(order, *args)


def basis_kernel(n_first, inv_ref, *refs):
    first, last, (bh_ref, bl_ref) = refs[:n_first], refs[n_first:-2], refs[-2:]
    per, _, block = first[0].shape
    ih, il = split(inv_ref[...])
    for t in range(n_first * per):
        ph, plo = split(jnp.concatenate([block_at(first, t)[...], block_at(last, t)[...]], axis=0))
        rows = slice(t * block, (t + 1) * block)
        bh_ref[rows, :], bl_ref[rows, :] = split(dot3(ih, il, ph, plo).T)


def basis_call(inv, pa, pb):
    refs = [*pa, *pb]
    blocks = len(pa) * pa[0].shape[0]
    _, width, block = pa[0].shape
    return pl.pallas_call(
        functools.partial(basis_kernel, len(pa)),
        in_specs=[VMEM] * (1 + len(refs)),
        out_specs=[VMEM, VMEM],
        out_shape=[pltpu.VMEM((blocks * block, 2 * width), BF16)] * 2,
        compiler_params=params(16),
        cost_estimate=cost(24 * width * width * block * blocks, 16 * width * block * blocks),
        name="basis",
    )(inv, *refs)


def cross_kernel(skip, inv_ref, *refs):
    raws, (out_ref, ch_ref, cl_ref, sq_ref) = refs[:-4], refs[-4:]
    size = skip + out_ref.shape[0]
    ih, il = split(inv_ref[skip:size, :size])
    rh, rl = split(jnp.concatenate([r[...] for r in raws], axis=0))
    cross = dot3(ih, il, rh, rl)
    out_ref[...] = cross
    ch_ref[...], cl_ref[...] = split(cross)
    sq_ref[...] = jnp.sum(cross * cross, axis=1, keepdims=True).T


def cross_call(inv, raws, skip):
    cols = raws[0].shape[1]
    rows = sum(r.shape[0] for r in raws) - skip
    return pl.pallas_call(
        functools.partial(cross_kernel, skip),
        in_specs=[VMEM] * (1 + len(raws)),
        out_specs=[VMEM] * 4,
        out_shape=[pltpu.VMEM((rows, cols), F32), pltpu.VMEM((rows, cols), BF16), pltpu.VMEM((rows, cols), BF16), shape((1, rows))],
        compiler_params=params(16),
        cost_estimate=cost(6 * rows * (rows + skip) * cols, 8 * rows * cols),
        name="cross",
    )(inv, *raws)


def store_rows(order_ref, place, buf, t, out_ref, sem):
    block = buf.shape[1]
    rows = pl.ds(pl.multiple_of(order_ref[place] * block, block), block)
    copy = pltpu.make_async_copy(buf.at[t], out_ref.at[rows, :], sem.at[t])
    copy.start()
    return copy


def momentum_kernel(order_ref, bh_ref, bl_ref, hi_ref, lo_ref, ch_ref, cl_ref, out_ref, buf, sem):
    blocks, block, _ = buf.shape
    copies = []
    for t in range(blocks):
        rows = slice(t * block, (t + 1) * block)
        prod = dot3(bh_ref[rows, :], bl_ref[rows, :], ch_ref[...], cl_ref[...])
        buf[t] = (hi_ref[rows, :].astype(F32) + lo_ref[rows, :].astype(F32)) - 0.5 * prod
        copies.append(store_rows(order_ref, t, buf, t, out_ref, sem))
    for copy in copies:
        copy.wait()


def momentum_call(order, bh, bl, hi, lo, ch, cl):
    rows, cols = hi.shape
    rank, blocks = bh.shape[1], order.shape[0]
    return pl.pallas_call(
        momentum_kernel,
        in_specs=[SMEM] + [VMEM] * 6,
        out_specs=HBM,
        out_shape=shape((rows, cols)),
        scratch_shapes=[pltpu.VMEM((blocks, rows // blocks, cols), F32), DMA((blocks,))],
        compiler_params=params(16),
        cost_estimate=cost(6 * rows * cols * rank, 8 * rows * cols),
        name="momentum_next",
    )(order, *in_vmem(bh, bl, hi, lo, ch, cl))


def update_kernel(factor, order_ref, bh_ref, bl_ref, c_ref, ch_ref, cl_ref, sq_ref, out_ref, qn_ref, buf, qbuf, sem, qsem):
    blocks, block, cols = buf.shape
    scale = 1.0 / (jnp.sqrt(sq_ref[...]) + 1e-08)
    copies = []
    step = cols // blocks
    for t in range(blocks):
        rows = slice(t * block, (t + 1) * block)
        bh, bl = split((bh_ref[rows, :].astype(F32) + bl_ref[rows, :].astype(F32)) * scale)
        prod = dot3(bh, bl, ch_ref[...], cl_ref[...])
        buf[t] = (factor * prod).astype(BF16)
        copies.append(store_rows(order_ref, t, buf, t, out_ref, sem))
        qbuf[t] = c_ref[:, t * step : (t + 1) * step].T * scale
        copy = pltpu.make_async_copy(qbuf.at[t], qn_ref.at[pl.ds(t * step, step), :], qsem.at[t])
        copy.start()
        copies.append(copy)
    for copy in copies:
        copy.wait()


def update_call(order, bh, bl, cross, ch, cl, sq, factor):
    rows, rank = bh.shape
    cols, blocks = cross.shape[1], order.shape[0]
    return pl.pallas_call(
        functools.partial(update_kernel, factor),
        in_specs=[SMEM] + [VMEM] * 6,
        out_specs=[HBM, HBM],
        out_shape=[shape((rows, cols), BF16), shape((cols, rank))],
        scratch_shapes=[
            pltpu.VMEM((blocks, rows // blocks, cols), BF16),
            pltpu.VMEM((blocks, cols // blocks, rank), F32),
            DMA((blocks,)),
            DMA((blocks,)),
        ],
        compiler_params=params(16),
        cost_estimate=cost(6 * rows * cols * rank, 8 * rows * cols),
        name="update",
    )(order, *in_vmem(bh, bl, cross, ch, cl), sq)


def fast(n_rows, n_cols, momentum_prev, gradient, q_prev):
    rank = q_prev.shape[1]
    width = rank // 2
    bits = n_cols.bit_length() - 1
    me = lax.axis_index("cols").astype(jnp.int32)
    masks = jnp.where(
        me % 2 == 0,
        jnp.array(position_masks(bits, 0), jnp.int32),
        jnp.array(position_masks(bits, 1), jnp.int32),
    )
    order = me ^ masks
    xor_order = me ^ jnp.arange(n_cols, dtype=jnp.int32)
    core = [(j, j ^ 1) for j in range(n_cols)]
    perms = pair_perms(bits)
    then = Order()

    def halve(k, r):
        n = k.shape[0] // 2
        return k[n:] + r[n:], k[:n] + r[:n]

    hi, lo, keep, send = then(lambda *x: first_call(*x, width), order, momentum_prev, gradient, q_prev)
    s, a = then(halve, keep, lax.ppermute(send, "cols", core))
    ra = lax.ppermute(s, "cols", perms[0])
    keep, send = then(lambda *x: rest_call(*x, rank - width, n_cols), hi, lo, q_prev)
    rb = lax.ppermute(send, "cols", core)
    s, a = then(halve, a, ra)
    a = then(jnp.add, a, lax.ppermute(s, "cols", perms[1]))
    ra = lax.ppermute(a, "cols", perms[1])

    def both_steps(a, ra, b, rb):
        s, b = halve(b, rb)
        a = join(a, ra)
        return join(a, s), a, b

    s, a, b = then(both_steps, a, ra, keep, rb)
    s = lax.ppermute(s, "cols", perms[0])
    n = a.shape[0]
    a = then(lambda a, s: join(a, s[:n]), a, s)
    pa = (a, lax.ppermute(a, "cols", core))
    s, b = then(halve, b, s[n:])
    state = {"inv": None, "b": b, "rb": lax.ppermute(s, "cols", perms[1])}
    later = [(jnp.add, perms[1]), (join, perms[0])]

    def step_b():
        if later:
            f, perm = later.pop(0)
            state["b"] = then(f, state["b"], state["rb"])
            state["rb"] = lax.ppermute(state["b"], "cols", perm)
        else:
            own = [state["b"], then(lambda r: r, state["rb"])]
            state["pb"] = (*own, *[lax.ppermute(x, "cols", core) for x in own])

    gram_stages = xor_stages(jnp.add, "rows", n_rows) + [(join, "cols", core)]
    sizes = [CHUNK] * (width // CHUNK)
    z = lax.axis_index("rows")
    ends = (z == 0) | (z == n_rows - 1)
    outer = [(i, i ^ 1) for i in range(n_rows)]
    inner = [(1, 2), (2, 1)]

    def raw(half):
        out = then(lambda p, h, l: raw_call(p, h, l, sizes), state["p" + half], hi, lo)
        for i, piece in enumerate(out):
            state[f"{half}{i}"] = piece

    def gram():
        if "gram" in state:
            state["gram"].step()
        else:
            x = then(gram_call, me.reshape(1), pa, state["pb"])
            state["gram"] = Sent(then, gram_stages, x)
        if not state["gram"].stages:
            x = state["gram"].x
            chips = [[(j, j ^ m) for j in range(n_cols)] for m in range(2, n_cols, 2)]
            state["pairs"] = [x] + [lax.ppermute(x, "cols", perm) for perm in chips]

    def factor():
        prev = [] if state["inv"] is None else [state["inv"]]
        n = len(state["pairs"])
        state["inv"] = then(lambda o, *g: chol_call(o, g[:n], *(g[n:] or [None])), xor_order, *state["pairs"], *prev)

    def basis():
        state["basis"] = then(basis_call, state["inv"], pa, state["pb"])

    def send_outer(new, old):
        both = [state[k] for k in (new, old) if k]
        x = then(lambda *p: jnp.where(ends, p[0], p[-1]) if len(p) > 1 else p[0], *both)
        state["outer"] = (new, old, lax.ppermute(x, "rows", outer))

    def take_outer():
        new, old, r = state["outer"]
        if new:
            state[new] = then(lambda x, r: jnp.where(ends, x, x + r), state[new], r)
        if old:
            state[old] = then(lambda x, r: jnp.where(ends, r, x), state[old], r)

    def send_inner(k):
        state["inner"] = (k, lax.ppermute(state[k], "rows", inner))

    def take_inner():
        k, r = state["inner"]
        state[k] = then(jnp.add, state[k], r)

    state["pa"] = pa
    names = [f"{half}{i}" for half in "ab" for i in range(len(sizes))]
    parts = names + [None, None]

    count = iter(range(len(parts)))

    def take():
        if "outer" in state:
            take_outer()
            del state["outer"]
        if "inner" in state:
            take_inner()
            del state["inner"]

    def slot():
        take()
        k = next(count)
        send_outer(parts[k], names[k - 2] if k > 1 else None)
        if 0 < k <= len(names):
            send_inner(names[k - 1])

    steps = {"raw_a": lambda: raw("a"), "raw_b": lambda: raw("b"), "b": step_b, "gram": gram}
    steps |= {"factor": factor, "basis": basis, "slot": slot, "take": take}
    for name in SCHEDULE:
        steps[name]()
    inv, (bh, bl) = state["inv"], state["basis"]
    raws = [state[name] for name in names]
    cross, ch, cl, sq = then(lambda i, *r: cross_call(i, r, 0), inv, *raws)
    sq = Sent(then, [(jnp.add, "cols", core)], sq).finish()
    chips = [[(j, j ^ m) for j in range(n_cols)] for m in range(2, n_cols, 2)]
    others = [lax.ppermute(sq, "cols", perm) for perm in chips]
    momentum_next = then(momentum_call, order, bh, bl, hi, lo, ch, cl)
    norm = then(lambda *x: sum(x[1:], x[0]), sq, *others)
    scale = momentum_prev.shape[0] * n_rows / rank**0.5
    update, q_next = then(lambda *x: update_call(*x, scale), order, bh, bl, cross, ch, cl, norm)
    return momentum_next, q_next, update


def plain(n_rows, n_cols, momentum_prev, gradient, q_prev):
    high = lax.Precision.HIGHEST
    dot = functools.partial(lax.dot_general, precision=high, preferred_element_type=F32)
    momentum = 0.95 * momentum_prev + gradient.astype(F32)
    power = lax.psum_scatter(dot(momentum, q_prev, NN), "cols", scatter_dimension=0, tiled=True)
    power = lax.all_gather(power, "cols", axis=0, tiled=True)
    tn = (((0,), (0,)), ((), ()))
    raw, gram = lax.psum((dot(momentum, power, tn), dot(power, power, tn)), "rows")
    chol = jnp.linalg.cholesky(gram)
    solve = functools.partial(lax.linalg.triangular_solve, chol, left_side=False, lower=True, transpose_a=True)
    basis, cross = solve(power), solve(raw)
    q_next = cross / (jnp.sqrt(lax.psum(jnp.sum(cross * cross, axis=0), "cols")) + 1e-08)
    momentum_next = momentum - 0.5 * dot(basis, cross, NT)
    factor = momentum_prev.shape[0] * n_rows / jnp.sqrt(jnp.float32(q_prev.shape[1]))
    return momentum_next, q_next, (factor * dot(basis, q_next, NT)).astype(BF16)


def solution(mesh):
    n_rows, n_cols = mesh.shape["rows"], mesh.shape["cols"]

    def body(momentum_prev, gradient, q_prev):
        rows, cols = momentum_prev.shape
        block = rows // n_cols
        fits = (
            n_rows == 4
            and n_cols == 8
            and block % 128 == 0
            and cols % 128 == 0
            and q_prev.shape[1] % (4 * CHUNK) == 0
        )
        return (fast if fits else plain)(n_rows, n_cols, momentum_prev, gradient, q_prev)

    in_specs = (P("rows", "cols"), P("rows", "cols"), P("cols", None))
    out_specs = (P("rows", "cols"), P("cols", None), P("rows", "cols"))
    return jax.shard_map(body, mesh=mesh, in_specs=in_specs, out_specs=out_specs, check_vma=False)
```
